256 devices in a mesh: lon: 64 (over z, x_hi, y), lat: 4 (over x_lo, core).
Axes of the slice: x: 4 (x_hi: 2, x_lo: 2; x = x_hi * 2 + x_lo), y: 4, z: 8, core: 2. Of those that a mesh axis runs over, the one named last changes fastest.
Arguments:
- control: float32 [4, 128, 1024, 128], P(None, 'lat', 'lon'), may hold values from -6 to 6
- observed: float32 [4, 128, 1024, 128], P(None, 'lat', 'lon'), may hold values from -6 to 6
- deviation: float32 [4, 128, 1024, 128], P(None, 'lat', 'lon'), may hold values from 0.3 to 3
- obs_weight: float32 [128, 1024], P('lat', 'lon'), may hold values from 0.5 to 2
- diffusivity: float32 [128, 1024], P('lat', 'lon'), may hold values from 0.05 to 0.24
- region_map: int32 [128, 1024], P('lat', 'lon'), may hold values from 0 to 15, as said below
- correlation: float32 [16, 4, 128, 128], replicated, as said below
Outputs:
- gradient: float32 [4, 128, 1024, 128], P(None, 'lat', 'lon')
The draws below stay inside these ranges and needn't reach their ends.
Inputs may be any that keep to these rules, and one draw needn't show every extreme that they name: `region_map`: constant on aligned tiles of 4 latitudes by 8 longitudes; every region appears somewhere. `correlation`: each matrix is a diagonal with entries from 0.8 to 1.2 plus independent entries of deviation about 0.6 / sqrt(128).
All inputs are finite; a program needn't handle non-finite values.
Results may differ from the reference program's by a relative error of at most 0.000057.
Values sent between devices are 32-bit elements; how exact they have to be, the bound alone decides.
A program may use at most 64 MiB of HBM per device.

```python
import math
import jax
import jax.numpy as jnp
from jax import lax

VARS = 4
LEVELS = 128
REGIONS = 16
PASSES = 4
NLAT = 128
NLON = 1024


def draw_region_map(key, part):
    tile_rows = NLAT // 4
    tile_cols = NLON // 8
    tiles = jax.random.randint(key, (tile_rows * tile_cols,), 0, REGIONS)
    leading = jax.random.permutation(jax.random.fold_in(key, 7), REGIONS).astype(jnp.int32)
    tiles = tiles.at[:REGIONS].set(leading)
    grid = tiles.reshape(tile_rows, tile_cols)
    return jnp.repeat(jnp.repeat(grid, 4, axis=0), 8, axis=1).astype(jnp.int32)


def draw_correlation(key, part):
    shape = (REGIONS, VARS, LEVELS, LEVELS)
    identity = jnp.eye(LEVELS, dtype=jnp.float32)[None, None]
    spread = 0.6 / LEVELS ** 0.5
    noise = jax.random.normal(key, shape, jnp.float32) * spread
    return (identity + noise).astype(jnp.float32)


def steps_of(own_key, shape, shards, least, top_value):
    def one(dim, blocks):
        heights = jax.random.uniform(jax.random.fold_in(jax.random.fold_in(own_key, 6), dim), (blocks,), jnp.float32, least / len(shards), top_value / len(shards))
        return jnp.repeat(jnp.exp(heights), shape[dim] // blocks).reshape((-1,) + (1,) * (len(shape) - dim - 1))

    factor_of = one(*shards[0])
    for cut in shards[1:]:
        factor_of = factor_of * one(*cut)
    return factor_of


def centred(rng, dims, scale, limit, shards=(), kind=jnp.bfloat16):
    entries = scale * jax.random.normal(rng, dims, jnp.float32)
    if shards:
        entries = entries * steps_of(rng, dims, shards, -0.22, 0.18)
    return jnp.clip(entries, -limit, limit).astype(kind)


def setup_inputs(seed: int = 0) -> dict:
    seeds = jax.random.split(jax.random.key(seed), 8)
    return {
        "control": centred(seeds[0], (VARS, NLAT, NLON, LEVELS), 1.0, 6.0, ((1, 4), (2, 64)), jnp.float32),
        "observed": centred(seeds[1], (VARS, NLAT, NLON, LEVELS), 1.0, 6.0, ((1, 4), (2, 64)), jnp.float32),
        "deviation": jnp.clip(jnp.exp(math.log(3.0) - 2.3025851 * jax.random.uniform(seeds[2], (VARS, NLAT, NLON, LEVELS), jnp.float32) ** steps_of(seeds[2], (VARS, NLAT, NLON, LEVELS), ((1, 4), (2, 64)), -0.2, 0.2)), 0.3, 3.0),
        "obs_weight": jnp.clip(jnp.exp(math.log(2.0) - 1.3862944 * jax.random.uniform(seeds[3], (NLAT, NLON), jnp.float32) ** steps_of(seeds[3], (NLAT, NLON), ((0, 4), (1, 64)), -0.2, 0.2)), 0.5, 2.0),
        "diffusivity": jnp.clip(0.05 + 0.19 * jax.random.uniform(seeds[4], (NLAT, NLON), jnp.float32) ** steps_of(seeds[4], (NLAT, NLON), ((0, 4), (1, 64)), -0.2, 0.2), 0.05, 0.24),
        "region_map": draw_region_map(jax.random.fold_in(seeds[7], 71), 0),
        "correlation": draw_correlation(jax.random.fold_in(seeds[7], 71), 0),
    }


def pad_grid(array, lat_axis, lon_axis):
    length = array.shape[lon_axis]
    first = lax.slice_in_dim(array, length - 1, length, axis=lon_axis)
    last = lax.slice_in_dim(array, 0, 1, axis=lon_axis)
    looped = jnp.concatenate([first, array, last], axis=lon_axis)
    widths = [(0, 0)] * array.ndim
    widths[lat_axis] = (1, 1)
    return jnp.pad(looped, widths)


def smooth(centre, lat_padded, lon_padded, padded_coef):
    middle = padded_coef[1:-1, 1:-1]
    upper_face = (0.5 * (middle + padded_coef[:-2, 1:-1]))[None, :, :, None]
    lower_face = (0.5 * (middle + padded_coef[2:, 1:-1]))[None, :, :, None]
    left_face = (0.5 * (middle + padded_coef[1:-1, :-2]))[None, :, :, None]
    right_face = (0.5 * (middle + padded_coef[1:-1, 2:]))[None, :, :, None]
    return (centre + upper_face * (lat_padded[:, :-2] - centre) + lower_face * (lat_padded[:, 2:] - centre)
            + left_face * (lon_padded[:, :, :-2] - centre) + right_face * (lon_padded[:, :, 2:] - centre))


def diffuse(field, padded_coef):
    for layer_pass in range(PASSES):
        padded = pad_grid(field, 1, 2)
        field = smooth(field, padded[:, :, 1:-1], padded[:, 1:-1, :], padded_coef)
    return field


def vertical(field, region_map, correlation, transpose):
    depth, lat_count, lon_count, levels = field.shape
    columns = field.transpose(1, 2, 0, 3).reshape(lat_count * lon_count, depth, levels)
    regions = region_map.reshape(lat_count * lon_count).astype(jnp.int32)
    blocks = lat_count * lon_count // 256

    def one_block(pair):
        block_cols, block_regions = pair
        matrices = correlation[block_regions]
        if transpose:
            return jnp.einsum('cvlm,cvl->cvm', matrices, block_cols, precision=lax.Precision.HIGHEST)
        return jnp.einsum('cvlm,cvm->cvl', matrices, block_cols, precision=lax.Precision.HIGHEST)

    result = lax.map(one_block, (columns.reshape(blocks, 256, depth, levels), regions.reshape(blocks, 256)))
    return result.reshape(lat_count, lon_count, depth, levels).transpose(2, 0, 1, 3)


def reference(control, observed, deviation, obs_weight, diffusivity, region_map, correlation):
    padded_coef = pad_grid(diffusivity, 0, 1)
    smoothed = diffuse(control, padded_coef)
    state = deviation * vertical(smoothed, region_map, correlation, False)
    weighted = deviation * (obs_weight[None, :, :, None] * (state - observed))
    back = vertical(weighted, region_map, correlation, True)
    return control + diffuse(back, padded_coef)
```

```python
import functools

import jax
import jax.numpy as jnp
from jax import lax
from jax.experimental import pallas as pl
from jax.experimental.pallas import tpu as pltpu
from jax.sharding import PartitionSpec as P

PASSES = 4
HALO = 4
MESH = pl.DeviceIdType.MESH
F32 = jnp.float32
BF16 = jnp.bfloat16

STEPS = ((-1, 0), (1, 0), (0, -1), (0, 1), (-1, -1), (1, -1), (-1, 1), (1, 1))
OPPOSITE = (1, 0, 3, 2, 7, 6, 5, 4)


def rolled(array, shift, axis):
    return pltpu.roll(array, shift % array.shape[axis], axis)


def lower_half(shape):
    return lax.broadcasted_iota(jnp.int32, shape, len(shape) - 2) < HALO


def pack_left(first, second):
    return jnp.where(lower_half(first.shape), first, rolled(second, HALO, 1))


def pack_right(first, second):
    return jnp.where(lower_half(first.shape), rolled(first, HALO, 1), second)


def unpack(from_right, from_left):
    low = lower_half(from_right.shape)
    first = jnp.where(low, from_right, rolled(from_left, HALO, 1))
    second = jnp.where(low, rolled(from_right, HALO, 1), from_left)
    return first, second


def halves(x):
    high = x.astype(BF16)
    return high, (x - high.astype(F32)).astype(BF16)


def kernel(
    lons, lats,
    ctl, obs, dev, wgt, dif, reg, cor, out,
    u1, u2, ct, ob, dv, corr, split, cx, cy, wb, regions, d_in, w_in, dt, dr,
    side_out, corner_out, side_in, corner_in,
    send_sem, recv_sem, dsend_sem, drecv_sem, small_sem, load_sem,
):
    variables, height, width, levels = ct.shape
    top, bottom = HALO, HALO + height
    me_lon, me_lat = lax.axis_index("lon"), lax.axis_index("lat")
    has_up, has_down = me_lat > 0, me_lat < lats - 1

    def neighbour(side):
        dlon, dlat = STEPS[side]
        return {"lon": lax.rem(me_lon + dlon + lons, lons), "lat": me_lat + dlat}

    def guarded(side, action):
        dlat = STEPS[side][1]
        if dlat == 0:
            action()
        else:
            pl.when(has_up if dlat < 0 else has_down)(action)

    barrier = pltpu.get_barrier_semaphore()
    for side in range(8):
        guarded(side, lambda side=side: pl.semaphore_signal(
            barrier, inc=1, device_id=neighbour(side), device_id_type=MESH))

    small = [
        pltpu.make_async_copy(dif, d_in, small_sem.at[0]),
        pltpu.make_async_copy(wgt, w_in, small_sem.at[1]),
        pltpu.make_async_copy(reg, regions, small_sem.at[2]),
    ]

    def own(ref, v):
        return ref.at[v, pl.ds(top, height), pl.ds(0, width)]

    def load(kind, v):
        source, target = (
            lambda: (ctl.at[v], own(u1, v)),
            lambda: (cor.at[:, v], corr.at[v]),
            lambda: (dev.at[v], dv.at[v]),
            lambda: (obs.at[v], ob.at[v]),
            lambda: (ctl.at[v], ct.at[v]),
        )[kind]()
        return pltpu.make_async_copy(source, target, load_sem.at[kind, v])

    for copy in small:
        copy.start()
    for kind in range(5):
        for v in range(variables):
            load(kind, v).start()

    def message(phase, v, side):
        if side < 2:
            source, target = side_out.at[phase, v, side], side_in.at[phase, v, OPPOSITE[side]]
        elif side < 4:
            row = 0 if side == 2 else height - HALO
            source = ctl.at[v, pl.ds(row, HALO)] if phase == 0 else u2.at[v, pl.ds(top + row, HALO), pl.ds(0, width)]
            row = bottom if side == 2 else 0
            target = (u1 if phase == 0 else u2).at[v, pl.ds(row, HALO), pl.ds(0, width)]
        else:
            source, target = corner_out.at[phase, v, side - 4], corner_in.at[phase, v, OPPOSITE[side] - 4]
        return pltpu.make_async_remote_copy(
            source, target, send_sem.at[phase, v, side], recv_sem.at[phase, v, OPPOSITE[side]],
            device_id=neighbour(side), device_id_type=MESH)

    def arrival(phase, v, side):
        if side < 2:
            target = side_in.at[phase, v, side]
        elif side < 4:
            target = (u1 if phase == 0 else u2).at[v, pl.ds(0 if side == 2 else bottom, HALO), pl.ds(0, width)]
        else:
            target = corner_in.at[phase, v, side - 4]
        return pltpu.make_async_remote_copy(
            target, target, send_sem.at[phase, v, side], recv_sem.at[phase, v, side],
            device_id=neighbour(side), device_id_type=MESH)

    def coefficients(side):
        dlon = STEPS[side][0]
        tile = pl.ds(0 if dlon <= 0 else 8, 8 if dlon else 16)
        return pltpu.make_async_remote_copy(
            dt.at[tile], dr.at[OPPOSITE[side], tile], dsend_sem.at[side], drecv_sem.at[OPPOSITE[side]],
            device_id=neighbour(side), device_id_type=MESH)

    def coefficients_in(side):
        dlon = STEPS[side][0]
        tile = pl.ds(0 if dlon >= 0 else 8, 8 if dlon else 16)
        return pltpu.make_async_remote_copy(
            dt.at[tile], dr.at[side, tile], dsend_sem.at[side], drecv_sem.at[side],
            device_id=neighbour(side), device_id_type=MESH)

    def pack(ref, phase, v):
        half = height // 2
        for side, columns, packer in ((0, pl.ds(0, 8), pack_left), (1, pl.ds(width - 8, 8), pack_right)):
            side_out[phase, v, side] = packer(
                ref[v, pl.ds(top, half), columns], ref[v, pl.ds(top + half, half), columns])
            corner_out[phase, v, side] = packer(
                ref[v, pl.ds(top, 2), columns], ref[v, pl.ds(top + 2, 2), columns])
            corner_out[phase, v, side + 2] = packer(
                ref[v, pl.ds(bottom - 4, 2), columns], ref[v, pl.ds(bottom - 2, 2), columns])

    def send(phase, v):
        for side in range(8):
            guarded(side, lambda side=side: message(phase, v, side).start())

    small[0].wait()
    small[1].wait()
    dt[...] = jnp.zeros_like(dt)
    dt[:, 0:height] = d_in[...]
    weight_t = w_in[...]

    load(0, 0).wait()
    pack(u1, 0, 0)

    pl.semaphore_wait(barrier, 2 + 3 * has_up.astype(jnp.int32) + 3 * has_down.astype(jnp.int32))

    for side in range(8):
        guarded(side, lambda side=side: coefficients(side).start())
    send(0, 0)

    @pl.loop(1, variables)
    def _(v):
        load(0, v).wait()
        pack(u1, 0, v)
        send(0, v)

    @pl.when(jnp.logical_not(has_up))
    def _():
        for ref in (u1, u2):
            ref[:, 0:top] = jnp.zeros((variables, HALO) + ref.shape[2:], F32)
        for side in (2, 4, 5):
            dr[side] = jnp.zeros(dr.shape[1:], F32)

    @pl.when(jnp.logical_not(has_down))
    def _():
        for ref in (u1, u2):
            ref[:, bottom:bottom + HALO] = jnp.zeros((variables, HALO) + ref.shape[2:], F32)
        for side in (3, 6, 7):
            dr[side] = jnp.zeros(dr.shape[1:], F32)

    for v in range(variables):
        load(1, v).wait()

        @pl.loop(0, corr.shape[1])
        def _(r):
            high, low = halves(corr[v, r])
            split[v, r, 0:levels] = high
            split[v, r, levels:2 * levels] = low

    for side in range(8):
        guarded(side, lambda side=side: coefficients_in(side).wait_recv())

    low = lower_half((8, 128))
    lane = lax.broadcasted_iota(jnp.int32, (24, 128), 1)

    def three(mid0, mid1, right, left):
        return jnp.concatenate([mid0, mid1, jnp.where(low, right, left)], axis=0)

    middle = three(dt[0:8], dt[8:16], dr[1, 0:8], dr[0, 8:16])
    above = three(dr[2, 0:8], dr[2, 8:16], dr[5, 0:8], dr[4, 8:16])
    below = three(dr[3, 0:8], dr[3, 8:16], dr[7, 0:8], dr[6, 8:16])
    grid = jnp.where(lane < top, rolled(above, HALO - height, 1), 0.0)
    grid = jnp.where((lane >= top) & (lane < bottom), rolled(middle, HALO, 1), grid)
    grid = jnp.where((lane >= bottom) & (lane < bottom + HALO), rolled(below, bottom, 1), grid)
    east = 0.5 * (grid + rolled(grid, -1, 0))
    south = 0.5 * (grid + rolled(grid, -1, 1))

    for r in range(height + 2 * HALO):
        cx[r] = jnp.broadcast_to(east[:, r:r + 1], (24, 128))
        cy[r] = jnp.broadcast_to(south[:, r:r + 1], (24, 128))
    for r in range(height):
        wb[r] = jnp.broadcast_to(weight_t[:, r:r + 1], (width, 128))

    keep_up = jnp.where(has_up, 1.0, 0.0).astype(F32)
    keep_down = jnp.where(has_down, 1.0, 0.0).astype(F32)

    def rows_step(ref, v, row, count, upper_flux, put, keep=None):
        here = ref[v, pl.ds(row, count)]
        after = ref[v, pl.ds(row + 1, count)]
        down = cy[pl.ds(row, count)] * (after - here)
        right = cx[pl.ds(row, count)] * (rolled(here, -1, 1) - here)
        up = upper_flux if count == 1 else jnp.concatenate([upper_flux, down[:-1]], axis=0)
        new = here + (down - up) + (right - rolled(right, 1, 1))
        if keep is not None:
            new = new * keep
        put(row, count, new)
        return down[count - 1:]

    def one_pass(ref, v, p, put):
        def store(row, count, new):
            ref[v, pl.ds(row, count)] = new

        flux = cy[p - 1:p] * (ref[v, p:p + 1] - ref[v, p - 1:p])
        if p < top:
            flux = rows_step(ref, v, p, top - p, flux, store, keep_up)

        def chunk(k, flux):
            return rows_step(ref, v, top + 4 * k, 4, flux, put or store)

        flux = lax.fori_loop(0, height // 4, chunk, flux)
        if p < top:
            rows_step(ref, v, bottom, top - p, flux, store, keep_down)

    def arrive(ref, phase, v):
        for side in range(8):
            guarded(side, lambda side=side: arrival(phase, v, side).wait_recv())
        columns = pl.ds(width, 8)
        half = height // 2
        first, second = unpack(side_in[phase, v, 1], side_in[phase, v, 0])
        ref[v, pl.ds(top, half), columns] = first
        ref[v, pl.ds(top + half, half), columns] = second

        @pl.when(has_up)
        def _():
            first, second = unpack(corner_in[phase, v, 1], corner_in[phase, v, 0])
            ref[v, pl.ds(0, 2), columns] = first
            ref[v, pl.ds(2, 2), columns] = second

        @pl.when(has_down)
        def _():
            first, second = unpack(corner_in[phase, v, 3], corner_in[phase, v, 2])
            ref[v, pl.ds(bottom, 2), columns] = first
            ref[v, pl.ds(bottom + 2, 2), columns] = second

    def joined(o):
        return o[:32, :levels] + (o[:32, levels:] + o[32:, :levels])

    small[2].wait()

    @pl.loop(0, variables)
    def _(v):
        arrive(u1, 0, v)
        for p in range(1, PASSES + 1):
            one_pass(u1, v, p, None)
        load(2, v).wait()
        load(3, v).wait()

        @pl.loop(0, height // 8)
        def _(pair):
            tiles = [(8 * pair + 4 * a, 8 * b) for a in range(2) for b in range(2)]

            def tile(ref, row, column):
                return ref[v, pl.ds(row, 4), pl.ds(column, 8)].reshape(32, levels)

            for row, column in tiles:
                matrix = split[v, regions[column, row]]
                lhs = jnp.concatenate(halves(tile(u1, top + row, column)), axis=0)
                state = joined(lax.dot_general(
                    lhs, matrix, (((1,), (1,)), ((), ())), preferred_element_type=F32))
                spread = tile(dv, row, column)
                weight = wb[pl.ds(row, 4), pl.ds(column, 8)].reshape(32, levels)
                weighted = spread * (weight * (spread * state - tile(ob, row, column)))
                lhs = jnp.concatenate(halves(weighted), axis=0)
                wide = jnp.concatenate([matrix[:levels], matrix[levels:]], axis=1)
                back = joined(jnp.dot(lhs, wide, preferred_element_type=F32))
                u2[v, pl.ds(top + row, 4), pl.ds(column, 8)] = back.reshape(4, 8, levels)

        pack(u2, 1, v)
        send(1, v)

    for v in range(variables):
        load(4, v).wait()

    @pl.loop(0, variables)
    def _(v):
        arrive(u2, 1, v)
        for side in (2, 3):
            guarded(side, lambda side=side: message(1, v, side).wait_send())
        for p in range(1, PASSES):
            one_pass(u2, v, p, None)

        def put(row, count, new):
            out[v, pl.ds(row - top, count)] = ct[v, pl.ds(row - top, count)] + new[:, :width]

        one_pass(u2, v, PASSES, put)

    @pl.loop(0, variables)
    def _(v):
        for phase in range(2):
            for side in range(8):
                if phase == 0 or side not in (2, 3):
                    guarded(side, lambda: message(phase, v, side).wait_send())

    for side in range(8):
        guarded(side, lambda side=side: coefficients(side).wait_send())


def on_device(lons, lats, control, observed, deviation, obs_weight, diffusivity, region_map, correlation):
    variables, height, width, levels = control.shape
    regions = correlation.shape[0]
    padded = (variables, height + 2 * HALO, width + 8, levels)
    anywhere = pl.BlockSpec(memory_space=pl.ANY)
    return pl.pallas_call(
        functools.partial(kernel, lons, lats),
        out_shape=jax.ShapeDtypeStruct(control.shape, F32),
        in_specs=[anywhere] * 7,
        out_specs=pl.BlockSpec(memory_space=pltpu.VMEM),
        scratch_shapes=[
            pltpu.VMEM(padded, F32),
            pltpu.VMEM(padded, F32),
            pltpu.VMEM(control.shape, F32),
            pltpu.VMEM(control.shape, F32),
            pltpu.VMEM(control.shape, F32),
            pltpu.VMEM((variables, regions, levels, levels), F32),
            pltpu.VMEM((variables, regions, 2 * levels, levels), BF16),
            pltpu.VMEM(padded[1:], F32),
            pltpu.VMEM(padded[1:], F32),
            pltpu.VMEM((height, width, levels), F32),
            pltpu.SMEM((width, height), jnp.int32),
            pltpu.VMEM((width, height), F32),
            pltpu.VMEM((width, height), F32),
            pltpu.VMEM((width, 128), F32),
            pltpu.VMEM((8, width, 128), F32),
            pltpu.VMEM((2, variables, 2, height // 2, 8, levels), F32),
            pltpu.VMEM((2, variables, 4, 2, 8, levels), F32),
            pltpu.VMEM((2, variables, 2, height // 2, 8, levels), F32),
            pltpu.VMEM((2, variables, 4, 2, 8, levels), F32),
            pltpu.SemaphoreType.DMA((2, variables, 8)),
            pltpu.SemaphoreType.DMA((2, variables, 8)),
            pltpu.SemaphoreType.DMA((8,)),
            pltpu.SemaphoreType.DMA((8,)),
            pltpu.SemaphoreType.DMA((3,)),
            pltpu.SemaphoreType.DMA((5, variables)),
        ],
        compiler_params=pltpu.CompilerParams(
            collective_id=0, has_side_effects=True, vmem_limit_bytes=60 * 2**20),
        cost_estimate=pl.CostEstimate(flops=10**9, bytes_accessed=8 * 2**20, transcendentals=0),
    )(control, observed, deviation, obs_weight.T, diffusivity.T, region_map.T, correlation)


def solution(mesh):
    field = P(None, "lat", "lon", None)
    cells = P("lat", "lon")
    return jax.shard_map(
        functools.partial(on_device, mesh.shape["lon"], mesh.shape["lat"]),
        mesh=mesh,
        in_specs=(field, field, field, cells, cells, cells, P()),
        out_specs=field,
        check_vma=False,
    )
```

```python
import functools

import jax
import jax.numpy as jnp
from jax import lax
from jax.experimental import pallas as pl
from jax.experimental.pallas import tpu as pltpu
from jax.sharding import PartitionSpec as P

PASSES = 4
HALO = 4
CHUNK = 8
GROUP = 4
MESH = pl.DeviceIdType.MESH
F32 = jnp.float32
BF16 = jnp.bfloat16

STEPS = ((-1, 0), (1, 0), (0, -1), (0, 1), (-1, -1), (1, -1), (-1, 1), (1, 1))
OPPOSITE = (1, 0, 3, 2, 7, 6, 5, 4)


def rolled(array, shift, axis):
    return pltpu.roll(array, shift % array.shape[axis], axis)


def lower_half(shape):
    return lax.broadcasted_iota(jnp.int32, shape, len(shape) - 2) < HALO


def pack_left(first, second):
    return jnp.where(lower_half(first.shape), first, rolled(second, HALO, 1))


def pack_right(first, second):
    return jnp.where(lower_half(first.shape), rolled(first, HALO, 1), second)


def corner_left(near, middle, far):
    place = lax.broadcasted_iota(jnp.int32, near.shape, 1)
    return jnp.where(place < 3, near, jnp.where(place < 5, rolled(middle, 3, 1), rolled(far, 5, 1)))


def corner_right(near, middle, far):
    place = lax.broadcasted_iota(jnp.int32, near.shape, 1)
    return jnp.where(place > 4, near, jnp.where(place > 2, rolled(middle, -3, 1), rolled(far, -5, 1)))


def halves(x):
    high = x.astype(BF16)
    return high, (x - high.astype(F32)).astype(BF16)


def kernel(
    lons, lats,
    ctl, obs, dev, wgt, dif, reg, cor, out,
    u1, u2, ct, ob, dv, corr, split, c0, cx, cy, wb, regions, d_in, w_in, dt, dr,
    side_out, corner_out, side_in, corner_in,
    send_sem, recv_sem, dsend_sem, drecv_sem, small_sem, load_sem,
):
    variables, height, width, levels = ct.shape
    top, bottom = HALO, HALO + height
    left, right = 8, 8 + width
    me_lon, me_lat = lax.axis_index("lon"), lax.axis_index("lat")
    has_up, has_down = me_lat > 0, me_lat < lats - 1

    def neighbour(side):
        dlon, dlat = STEPS[side]
        return {"lon": lax.rem(me_lon + dlon + lons, lons), "lat": me_lat + dlat}

    def guarded(side, action):
        dlat = STEPS[side][1]
        if dlat == 0:
            action()
        else:
            pl.when(has_up if dlat < 0 else has_down)(action)

    barrier = pltpu.get_barrier_semaphore()
    for side in range(8):
        guarded(side, lambda side=side: pl.semaphore_signal(
            barrier, inc=1, device_id=neighbour(side), device_id_type=MESH))

    small = [
        pltpu.make_async_copy(dif, d_in, small_sem.at[0]),
        pltpu.make_async_copy(wgt, w_in, small_sem.at[1]),
        pltpu.make_async_copy(reg, regions, small_sem.at[2]),
    ]

    def own(ref, v):
        return ref.at[v, pl.ds(top, height), pl.ds(left, width)]

    def load(kind, v):
        source, target = (
            lambda: (ctl.at[v], own(u1, v)),
            lambda: (cor.at[:, v], corr.at[v]),
            lambda: (dev.at[v], dv.at[v]),
            lambda: (obs.at[v], ob.at[v]),
            lambda: (ctl.at[v], ct.at[v]),
        )[kind]()
        return pltpu.make_async_copy(source, target, load_sem.at[kind, v])

    for copy in small:
        copy.start()
    for kind in range(5):
        for v in range(variables):
            load(kind, v).start()

    def message(phase, v, side):
        if side < 2:
            source, target = side_out.at[phase, v, side], side_in.at[phase, v, OPPOSITE[side]]
        elif side < 4:
            row = 0 if side == 2 else height - HALO
            source = ctl.at[v, pl.ds(row, HALO)] if phase == 0 else u2.at[v, pl.ds(top + row, HALO), pl.ds(left, width)]
            row = bottom if side == 2 else 0
            target = (u1 if phase == 0 else u2).at[v, pl.ds(row, HALO), pl.ds(left, width)]
        else:
            source, target = corner_out.at[phase, v, side - 4], corner_in.at[phase, v, OPPOSITE[side] - 4]
        return pltpu.make_async_remote_copy(
            source, target, send_sem.at[phase, v, side], recv_sem.at[phase, v, OPPOSITE[side]],
            device_id=neighbour(side), device_id_type=MESH)

    def arrival(phase, v, side):
        if side < 2:
            target = side_in.at[phase, v, side]
        elif side < 4:
            target = (u1 if phase == 0 else u2).at[v, pl.ds(0 if side == 2 else bottom, HALO), pl.ds(left, width)]
        else:
            target = corner_in.at[phase, v, side - 4]
        return pltpu.make_async_remote_copy(
            target, target, send_sem.at[phase, v, side], recv_sem.at[phase, v, side],
            device_id=neighbour(side), device_id_type=MESH)

    def coefficients(side):
        dlon = STEPS[side][0]
        tile = pl.ds(0 if dlon <= 0 else 8, 8 if dlon else 16)
        return pltpu.make_async_remote_copy(
            dt.at[tile], dr.at[OPPOSITE[side], tile], dsend_sem.at[side], drecv_sem.at[OPPOSITE[side]],
            device_id=neighbour(side), device_id_type=MESH)

    def coefficients_in(side):
        dlon = STEPS[side][0]
        tile = pl.ds(0 if dlon >= 0 else 8, 8 if dlon else 16)
        return pltpu.make_async_remote_copy(
            dt.at[tile], dr.at[side, tile], dsend_sem.at[side], drecv_sem.at[side],
            device_id=neighbour(side), device_id_type=MESH)

    def pack(ref, phase, v):
        half = height // 2
        for side, column, packer, corner in ((0, left, pack_left, corner_left), (1, right - 8, pack_right, corner_right)):
            columns = pl.ds(column, 8)
            side_out[phase, v, side] = packer(
                ref[v, pl.ds(top, half), columns], ref[v, pl.ds(top + half, half), columns])
            for place, rows in ((side, (top, top + 1, top + 2)), (side + 2, (bottom - 1, bottom - 2, bottom - 3))):
                corner_out[phase, v, place] = corner(*(ref[v, pl.ds(row, 1), columns] for row in rows))[0]

    def send(phase, v):
        for side in range(8):
            guarded(side, lambda side=side: message(phase, v, side).start())

    small[0].wait()
    small[1].wait()
    dt[...] = jnp.zeros_like(dt)
    dt[:, 0:height] = d_in[...]
    weight_t = w_in[...]

    load(0, 0).wait()
    pack(u1, 0, 0)

    pl.semaphore_wait(barrier, 2 + 3 * has_up.astype(jnp.int32) + 3 * has_down.astype(jnp.int32))

    for side in range(8):
        guarded(side, lambda side=side: coefficients(side).start())
    send(0, 0)

    @pl.loop(1, variables)
    def _(v):
        load(0, v).wait()
        pack(u1, 0, v)
        send(0, v)

    @pl.when(jnp.logical_not(has_up))
    def _():
        for ref in (u1, u2):
            ref[:, 0:top] = jnp.zeros((variables, HALO) + ref.shape[2:], F32)
        for side in (2, 4, 5):
            dr[side] = jnp.zeros(dr.shape[1:], F32)

    @pl.when(jnp.logical_not(has_down))
    def _():
        for ref in (u1, u2):
            ref[:, bottom:bottom + HALO] = jnp.zeros((variables, HALO) + ref.shape[2:], F32)
        for side in (3, 6, 7):
            dr[side] = jnp.zeros(dr.shape[1:], F32)

    for v in range(variables):
        load(1, v).wait()

        @pl.loop(0, corr.shape[1])
        def _(r):
            high, low = halves(corr[v, r])
            split[v, r, 0:levels] = high
            split[v, r, levels:2 * levels] = low

    for side in range(8):
        guarded(side, lambda side=side: coefficients_in(side).wait_recv())

    lane = lax.broadcasted_iota(jnp.int32, (width + 16, 128), 1)

    def across(own, from_left, from_right):
        return jnp.concatenate([from_left[8:16], own[0:16], from_right[0:8]], axis=0)

    middle = across(dt, dr[0], dr[1])
    above = across(dr[2], dr[4], dr[5])
    below = across(dr[3], dr[6], dr[7])
    grid = jnp.where(lane < top, rolled(above, HALO - height, 1), 0.0)
    grid = jnp.where((lane >= top) & (lane < bottom), rolled(middle, HALO, 1), grid)
    grid = jnp.where((lane >= bottom) & (lane < bottom + HALO), rolled(below, bottom, 1), grid)
    east = 0.5 * (grid + rolled(grid, -1, 0))
    south = 0.5 * (grid + rolled(grid, -1, 1))
    rest = 1.0 - (east + rolled(east, 1, 0)) - (south + rolled(south, 1, 1))
    first_row = jnp.where(has_up, 0, top)
    last_row = jnp.where(has_down, bottom + HALO, bottom)
    inside = (lane >= first_row) & (lane < last_row)
    rest = jnp.where(inside, rest, 0.0)
    east = jnp.where(inside, east, 0.0)
    south = jnp.where(inside & (lane < last_row - 1), south, 0.0)

    for r in range(height + 2 * HALO):
        for coefficient, ref in ((rest, c0), (east, cx), (south, cy)):
            ref[r] = jnp.broadcast_to(coefficient[:, r:r + 1], ref.shape[1:])
    for r in range(height):
        wb[r] = jnp.broadcast_to(weight_t[:, r:r + 1], (width, 128))

    def rows_step(ref, v, row, count, above, first, last, put):
        here_columns = pl.ds(first, last - first)
        block = ref[v, pl.ds(row, count + 1), here_columns]
        here = block[:count]
        up = above if count == 1 else jnp.concatenate([above, here[:-1]], axis=0)
        rows = pl.ds(row, count)
        faces = cy[pl.ds(row - 1, count + 1), here_columns]
        new = c0[rows, here_columns] * here + (faces[1:] * block[1:] + faces[:-1] * up)
        new = new + (cx[rows, here_columns] * ref[v, rows, pl.ds(first + 1, last - first)]
                     + cx[rows, pl.ds(first - 1, last - first)] * ref[v, rows, pl.ds(first - 1, last - first)])
        put(row, count, new)
        return here[count - 1:]

    def one_pass(ref, v, p, put):
        first, last = (left - HALO, right + HALO) if p < PASSES else (left, right)
        here_columns = pl.ds(first, last - first)

        def store(row, count, new):
            ref[v, pl.ds(row, count), here_columns] = new

        above = ref[v, p - 1:p, here_columns]
        if p < PASSES:
            above = rows_step(ref, v, p, top - p, above, first, last, store)

        def chunk(k, above):
            return rows_step(ref, v, top + CHUNK * k, CHUNK, above, first, last, put or store)

        above = lax.fori_loop(0, height // CHUNK, chunk, above)
        if p < PASSES:
            rows_step(ref, v, bottom, top - p, above, first, last, store)

    def arrive(ref, phase, v):
        for side in range(8):
            guarded(side, lambda side=side: arrival(phase, v, side).wait_recv())
        half = height // 2
        to_left, to_right = pl.ds(left - 8, 8), pl.ds(right, 8)
        from_left, from_right = side_in[phase, v, 0], side_in[phase, v, 1]
        ref[v, pl.ds(top, half), to_left] = rolled(from_left, HALO, 1)
        ref[v, pl.ds(top + half, half), to_left] = from_left
        ref[v, pl.ds(top, half), to_right] = from_right
        ref[v, pl.ds(top + half, half), to_right] = rolled(from_right, HALO, 1)

        def corners(place, rows):
            for n, row in enumerate(rows):
                turn = (0, 3, 5)[n]
                ref[v, row, to_left] = rolled(corner_in[phase, v, place], turn, 0)
                ref[v, row, to_right] = rolled(corner_in[phase, v, place + 1], -turn, 0)

        pl.when(has_up)(lambda: corners(0, (top - 1, top - 2, top - 3)))
        pl.when(has_down)(lambda: corners(2, (bottom, bottom + 1, bottom + 2)))

    def joined(o):
        return o[:32, :levels] + (o[:32, levels:] + o[32:, :levels])

    small[2].wait()

    @pl.loop(0, variables)
    def _(v):
        arrive(u1, 0, v)
        for p in range(1, PASSES + 1):
            one_pass(u1, v, p, None)
        load(2, v).wait()
        load(3, v).wait()

        def tile(ref, row, column):
            return ref[v, pl.ds(row, 4), pl.ds(column, 8)].reshape(32, levels)

        def forward(row, column):
            matrix = split[v, regions[column, row]]
            lhs = jnp.concatenate(halves(tile(u1, top + row, left + column)), axis=0)
            return lax.dot_general(lhs, matrix, (((1,), (1,)), ((), ())), preferred_element_type=F32)

        def adjoint(row, column, product):
            matrix = split[v, regions[column, row]]
            spread = tile(dv, row, column)
            weight = wb[pl.ds(row, 4), pl.ds(column, 8)].reshape(32, levels)
            weighted = spread * (weight * (spread * joined(product) - tile(ob, row, column)))
            lhs = jnp.concatenate(halves(weighted), axis=0)
            wide = jnp.concatenate([matrix[:levels], matrix[levels:]], axis=1)
            return jnp.dot(lhs, wide, preferred_element_type=F32)

        def finish(row, column, product):
            u2[v, pl.ds(top + row, 4), pl.ds(left + column, 8)] = joined(product).reshape(4, 8, levels)

        tiles = [(4 * a, 8 * b) for a in range(height // 4) for b in range(width // 8)]
        groups = [tiles[n:n + GROUP] for n in range(0, len(tiles), GROUP)]
        forwards, adjoints = {}, {}
        for n in range(len(groups) + 2):
            if n < len(groups):
                forwards[n] = [forward(*t) for t in groups[n]]
            if 0 <= n - 1 < len(groups):
                adjoints[n - 1] = [adjoint(*t, o) for t, o in zip(groups[n - 1], forwards.pop(n - 1))]
            if n >= 2:
                for t, o in zip(groups[n - 2], adjoints.pop(n - 2)):
                    finish(*t, o)

        pack(u2, 1, v)
        send(1, v)

    for v in range(variables):
        load(4, v).wait()

    @pl.loop(0, variables)
    def _(v):
        arrive(u2, 1, v)
        for side in (2, 3):
            guarded(side, lambda side=side: message(1, v, side).wait_send())
        for p in range(1, PASSES):
            one_pass(u2, v, p, None)

        def put(row, count, new):
            out[v, pl.ds(row - top, count)] = ct[v, pl.ds(row - top, count)] + new

        one_pass(u2, v, PASSES, put)

    @pl.loop(0, variables)
    def _(v):
        for phase in range(2):
            for side in range(8):
                if phase == 0 or side not in (2, 3):
                    guarded(side, lambda: message(phase, v, side).wait_send())

    for side in range(8):
        guarded(side, lambda side=side: coefficients(side).wait_send())


def on_device(lons, lats, control, observed, deviation, obs_weight, diffusivity, region_map, correlation):
    variables, height, width, levels = control.shape
    regions = correlation.shape[0]
    padded = (variables, height + 2 * HALO, width + 16, levels)
    in_hbm = pl.BlockSpec(memory_space=pltpu.HBM)
    return pl.pallas_call(
        functools.partial(kernel, lons, lats),
        out_shape=jax.ShapeDtypeStruct(control.shape, F32),
        in_specs=[in_hbm] * 7,
        out_specs=pl.BlockSpec(memory_space=pltpu.VMEM),
        scratch_shapes=[
            pltpu.VMEM(padded, F32),
            pltpu.VMEM(padded, F32),
            pltpu.VMEM(control.shape, F32),
            pltpu.VMEM(control.shape, F32),
            pltpu.VMEM(control.shape, F32),
            pltpu.VMEM((variables, regions, levels, levels), F32),
            pltpu.VMEM((variables, regions, 2 * levels, levels), BF16),
            pltpu.VMEM(padded[1:], F32),
            pltpu.VMEM(padded[1:], F32),
            pltpu.VMEM(padded[1:], F32),
            pltpu.VMEM((height, width, levels), F32),
            pltpu.SMEM((width, height), jnp.int32),
            pltpu.VMEM((width, height), F32),
            pltpu.VMEM((width, height), F32),
            pltpu.VMEM((width, 128), F32),
            pltpu.VMEM((8, width, 128), F32),
            pltpu.VMEM((2, variables, 2, height // 2, 8, levels), F32),
            pltpu.VMEM((2, variables, 4, 8, levels), F32),
            pltpu.VMEM((2, variables, 2, height // 2, 8, levels), F32),
            pltpu.VMEM((2, variables, 4, 8, levels), F32),
            pltpu.SemaphoreType.DMA((2, variables, 8)),
            pltpu.SemaphoreType.DMA((2, variables, 8)),
            pltpu.SemaphoreType.DMA((8,)),
            pltpu.SemaphoreType.DMA((8,)),
            pltpu.SemaphoreType.DMA((3,)),
            pltpu.SemaphoreType.DMA((5, variables)),
        ],
        compiler_params=pltpu.CompilerParams(
            collective_id=0, has_side_effects=True, vmem_limit_bytes=52 * 2**20),
        cost_estimate=pl.CostEstimate(flops=10**9, bytes_accessed=8 * 2**20, transcendentals=0),
    )(control, observed, deviation, obs_weight.T, diffusivity.T, region_map.T, correlation)


def solution(mesh):
    field = P(None, "lat", "lon", None)
    cells = P("lat", "lon")
    return jax.shard_map(
        functools.partial(on_device, mesh.shape["lon"], mesh.shape["lat"]),
        mesh=mesh,
        in_specs=(field, field, field, cells, cells, cells, P()),
        out_specs=field,
        check_vma=False,
    )
```

```python
import functools

import jax
import jax.numpy as jnp
from jax import lax
from jax.experimental import pallas as pl
from jax.experimental.pallas import tpu as pltpu
from jax.sharding import PartitionSpec as P

PASSES = 4
HALO = 4
CHUNK = 16
GROUP = 8
MESH = pl.DeviceIdType.MESH
F32 = jnp.float32
BF16 = jnp.bfloat16

STEPS = ((-1, 0), (1, 0), (0, -1), (0, 1), (-1, -1), (1, -1), (-1, 1), (1, 1))
OPPOSITE = (1, 0, 3, 2, 7, 6, 5, 4)


def rolled(array, shift, axis):
    return pltpu.roll(array, shift % array.shape[axis], axis)


def lower_half(shape):
    return lax.broadcasted_iota(jnp.int32, shape, len(shape) - 2) < HALO


def pack_left(first, second):
    return jnp.where(lower_half(first.shape), first, rolled(second, HALO, 1))


def pack_right(first, second):
    return jnp.where(lower_half(first.shape), rolled(first, HALO, 1), second)


def corner_left(near, middle, far):
    place = lax.broadcasted_iota(jnp.int32, near.shape, 1)
    return jnp.where(place < 3, near, jnp.where(place < 5, rolled(middle, 3, 1), rolled(far, 5, 1)))


def corner_right(near, middle, far):
    place = lax.broadcasted_iota(jnp.int32, near.shape, 1)
    return jnp.where(place > 4, near, jnp.where(place > 2, rolled(middle, -3, 1), rolled(far, -5, 1)))


def halves(x):
    high = x.astype(BF16)
    return high, (x - high.astype(F32)).astype(BF16)


def kernel(
    lons, lats,
    ctl, obs, dev, pair, reg, cor, out,
    u1, u2, ct, ob, dv, corr, split, c0, cx, cw, cy, wb, regions, dt, dr,
    side_out, corner_out, side_in, corner_in,
    send_sem, recv_sem, dsend_sem, drecv_sem, small_sem, load_sem,
):
    variables, height, width, levels = ct.shape
    top, bottom = HALO, HALO + height
    left, right = 8, 8 + width
    me_lon, me_lat = lax.axis_index("lon"), lax.axis_index("lat")
    has_up, has_down = me_lat > 0, me_lat < lats - 1

    def neighbour(side):
        dlon, dlat = STEPS[side]
        return {"lon": lax.rem(me_lon + dlon + lons, lons), "lat": me_lat + dlat}

    def guarded(side, action):
        dlat = STEPS[side][1]
        if dlat == 0:
            action()
        else:
            pl.when(has_up if dlat < 0 else has_down)(action)

    barrier = pltpu.get_barrier_semaphore()
    for side in range(8):
        guarded(side, lambda side=side: pl.semaphore_signal(
            barrier, inc=1, device_id=neighbour(side), device_id_type=MESH))

    region_copy = pltpu.make_async_copy(reg, regions, small_sem.at[0])

    def own(ref, v):
        return ref.at[v, pl.ds(top, height), pl.ds(left, width)]

    def load(kind, v):
        source, target = (
            lambda: (ctl.at[v], own(u1, v)),
            lambda: (cor.at[:, v], corr.at[v]),
            lambda: (dev.at[v], dv.at[v]),
            lambda: (obs.at[v], ob.at[v]),
            lambda: (ctl.at[v], ct.at[v]),
        )[kind]()
        return pltpu.make_async_copy(source, target, load_sem.at[kind, v])

    for kind in range(4):
        for v in range(variables):
            load(kind, v).start()
    region_copy.start()

    def message(phase, v, side):
        if side < 2:
            source, target = side_out.at[phase, v, side], side_in.at[phase, v, OPPOSITE[side]]
        elif side < 4:
            row = 0 if side == 2 else height - HALO
            source = ctl.at[v, pl.ds(row, HALO)] if phase == 0 else u2.at[v, pl.ds(top + row, HALO), pl.ds(left, width)]
            row = bottom if side == 2 else 0
            target = (u1 if phase == 0 else u2).at[v, pl.ds(row, HALO), pl.ds(left, width)]
        else:
            source, target = corner_out.at[phase, v, side - 4], corner_in.at[phase, v, OPPOSITE[side] - 4]
        return pltpu.make_async_remote_copy(
            source, target, send_sem.at[phase, v, side], recv_sem.at[phase, v, OPPOSITE[side]],
            device_id=neighbour(side), device_id_type=MESH)

    def arrival(phase, v, side):
        if side < 2:
            target = side_in.at[phase, v, side]
        elif side < 4:
            target = (u1 if phase == 0 else u2).at[v, pl.ds(0 if side == 2 else bottom, HALO), pl.ds(left, width)]
        else:
            target = corner_in.at[phase, v, side - 4]
        return pltpu.make_async_remote_copy(
            target, target, send_sem.at[phase, v, side], recv_sem.at[phase, v, side],
            device_id=neighbour(side), device_id_type=MESH)

    def coefficients(side):
        dlon = STEPS[side][0]
        tile = pl.ds(0 if dlon <= 0 else 8, 8 if dlon else 16)
        return pltpu.make_async_remote_copy(
            dt.at[tile], dr.at[OPPOSITE[side], tile], dsend_sem.at[side], drecv_sem.at[OPPOSITE[side]],
            device_id=neighbour(side), device_id_type=MESH)

    def coefficients_in(side):
        dlon = STEPS[side][0]
        tile = pl.ds(0 if dlon >= 0 else 8, 8 if dlon else 16)
        return pltpu.make_async_remote_copy(
            dt.at[tile], dr.at[side, tile], dsend_sem.at[side], drecv_sem.at[side],
            device_id=neighbour(side), device_id_type=MESH)

    def pack(ref, phase, v):
        half = height // 2
        for side, column, packer, corner in ((0, left, pack_left, corner_left), (1, right - 8, pack_right, corner_right)):
            columns = pl.ds(column, 8)
            side_out[phase, v, side] = packer(
                ref[v, pl.ds(top, half), columns], ref[v, pl.ds(top + half, half), columns])
            for place, rows in ((side, (top, top + 1, top + 2)), (side + 2, (bottom - 1, bottom - 2, bottom - 3))):
                corner_out[phase, v, place] = corner(*(ref[v, pl.ds(row, 1), columns] for row in rows))[0]

    def send(phase, v):
        for side in (4, 5, 6, 7, 2, 3, 0, 1):
            guarded(side, lambda side=side: message(phase, v, side).start())

    dt[...] = jnp.zeros_like(dt)
    dt[:, 0:height] = pair[0:width]
    weight_t = pair[width:2 * width]

    load(0, 0).wait()
    pack(u1, 0, 0)

    pl.semaphore_wait(barrier, 2 + 3 * has_up.astype(jnp.int32) + 3 * has_down.astype(jnp.int32))

    for side in range(8):
        guarded(side, lambda side=side: coefficients(side).start())
    send(0, 0)

    @pl.loop(1, variables)
    def _(v):
        load(0, v).wait()
        pack(u1, 0, v)
        send(0, v)

    @pl.when(jnp.logical_not(has_up))
    def _():
        for ref in (u1, u2):
            ref[:, 0:top] = jnp.zeros((variables, HALO) + ref.shape[2:], F32)
        for side in (2, 4, 5):
            dr[side] = jnp.zeros(dr.shape[1:], F32)

    @pl.when(jnp.logical_not(has_down))
    def _():
        for ref in (u1, u2):
            ref[:, bottom:bottom + HALO] = jnp.zeros((variables, HALO) + ref.shape[2:], F32)
        for side in (3, 6, 7):
            dr[side] = jnp.zeros(dr.shape[1:], F32)

    for v in range(variables):
        load(1, v).wait()

        @pl.loop(0, corr.shape[1])
        def _(r):
            high, low = halves(corr[v, r])
            split[v, r, 0:levels] = high
            split[v, r, levels:2 * levels] = low

    for side in range(8):
        guarded(side, lambda side=side: coefficients_in(side).wait_recv())

    lane = lax.broadcasted_iota(jnp.int32, (width + 16, 128), 1)

    def across(own, from_left, from_right):
        return jnp.concatenate([from_left[8:16], own[0:16], from_right[0:8]], axis=0)

    middle = across(dt, dr[0], dr[1])
    above = across(dr[2], dr[4], dr[5])
    below = across(dr[3], dr[6], dr[7])
    grid = jnp.where(lane < top, rolled(above, HALO - height, 1), 0.0)
    grid = jnp.where((lane >= top) & (lane < bottom), rolled(middle, HALO, 1), grid)
    grid = jnp.where((lane >= bottom) & (lane < bottom + HALO), rolled(below, bottom, 1), grid)
    east = 0.5 * (grid + rolled(grid, -1, 0))
    south = 0.5 * (grid + rolled(grid, -1, 1))
    rest = 1.0 - (east + rolled(east, 1, 0)) - (south + rolled(south, 1, 1))
    first_row = jnp.where(has_up, 0, top)
    last_row = jnp.where(has_down, bottom + HALO, bottom)
    inside = (lane >= first_row) & (lane < last_row)
    rest = jnp.where(inside, rest, 0.0)
    east = jnp.where(inside, east, 0.0)
    south = jnp.where(inside & (lane < last_row - 1), south, 0.0)

    kept = width + 2 * HALO
    start = left - HALO
    west = rolled(east, 1 - start, 0)[:kept]
    rest, east, south = (rolled(x, -start, 0)[:kept] for x in (rest, east, south))

    for r in range(height + 2 * HALO):
        for coefficient, ref in ((rest, c0), (east, cx), (west, cw), (south, cy)):
            ref[r] = jnp.broadcast_to(coefficient[:, r:r + 1], ref.shape[1:])
    for r in range(height):
        wb[r] = jnp.broadcast_to(weight_t[:, r:r + 1], (width, 128))

    def rows_step(ref, v, row, count, above, first, last, put):
        here_columns = pl.ds(first, last - first)
        kept_columns = pl.ds(first - start, last - first)
        block = ref[v, pl.ds(row, count + 1), here_columns]
        here = block[:count]
        up = above if count == 1 else jnp.concatenate([above, here[:-1]], axis=0)
        rows = pl.ds(row, count)
        faces = cy[pl.ds(row - 1, count + 1), kept_columns]
        new = c0[rows, kept_columns] * here + (faces[1:] * block[1:] + faces[:-1] * up)
        new = new + (cx[rows, kept_columns] * ref[v, rows, pl.ds(first + 1, last - first)]
                     + cw[rows, kept_columns] * ref[v, rows, pl.ds(first - 1, last - first)])
        put(row, count, new)
        return here[count - 1:]

    def one_pass(ref, v, p, put):
        first, last = (left - HALO, right + HALO) if p < PASSES else (left, right)
        here_columns = pl.ds(first, last - first)

        def store(row, count, new):
            ref[v, pl.ds(row, count), here_columns] = new

        above = ref[v, p - 1:p, here_columns]
        if p < PASSES:
            above = rows_step(ref, v, p, top - p, above, first, last, store)

        def chunk(k, above):
            return rows_step(ref, v, top + CHUNK * k, CHUNK, above, first, last, put or store)

        above = lax.fori_loop(0, height // CHUNK, chunk, above)
        if p < PASSES:
            rows_step(ref, v, bottom, top - p, above, first, last, store)

    def arrive(ref, phase, v):
        for side in range(8):
            guarded(side, lambda side=side: arrival(phase, v, side).wait_recv())
        half = height // 2
        to_left, to_right = pl.ds(left - 8, 8), pl.ds(right, 8)
        from_left, from_right = side_in[phase, v, 0], side_in[phase, v, 1]
        ref[v, pl.ds(top, half), to_left] = rolled(from_left, HALO, 1)
        ref[v, pl.ds(top + half, half), to_left] = from_left
        ref[v, pl.ds(top, half), to_right] = from_right
        ref[v, pl.ds(top + half, half), to_right] = rolled(from_right, HALO, 1)

        def corners(place, rows):
            for n, row in enumerate(rows):
                turn = (0, 3, 5)[n]
                ref[v, row, to_left] = rolled(corner_in[phase, v, place], turn, 0)
                ref[v, row, to_right] = rolled(corner_in[phase, v, place + 1], -turn, 0)

        pl.when(has_up)(lambda: corners(0, (top - 1, top - 2, top - 3)))
        pl.when(has_down)(lambda: corners(2, (bottom, bottom + 1, bottom + 2)))

    def joined(o):
        return o[:32, :levels] + (o[:32, levels:] + o[32:, :levels])

    region_copy.wait()
    for v in range(variables):
        load(4, v).start()

    @pl.loop(0, variables)
    def _(v):
        arrive(u1, 0, v)
        for p in range(1, PASSES + 1):
            one_pass(u1, v, p, None)
        load(2, v).wait()
        load(3, v).wait()

        def tile(ref, row, column):
            return ref[v, pl.ds(row, 4), pl.ds(column, 8)].reshape(32, levels)

        def forward(row, column):
            matrix = split[v, regions[column, row]]
            lhs = jnp.concatenate(halves(tile(u1, top + row, left + column)), axis=0)
            return lax.dot_general(lhs, matrix, (((1,), (1,)), ((), ())), preferred_element_type=F32)

        def adjoint(row, column, product):
            matrix = split[v, regions[column, row]]
            spread = tile(dv, row, column)
            weight = wb[pl.ds(row, 4), pl.ds(column, 8)].reshape(32, levels)
            weighted = spread * (weight * (spread * joined(product) - tile(ob, row, column)))
            lhs = jnp.concatenate(halves(weighted), axis=0)
            wide = jnp.concatenate([matrix[:levels], matrix[levels:]], axis=1)
            return jnp.dot(lhs, wide, preferred_element_type=F32)

        def finish(row, column, product):
            u2[v, pl.ds(top + row, 4), pl.ds(left + column, 8)] = joined(product).reshape(4, 8, levels)

        tiles = [(4 * a, 8 * b) for a in range(height // 4) for b in range(width // 8)]
        groups = [tiles[n:n + GROUP] for n in range(0, len(tiles), GROUP)]
        forwards, adjoints = {}, {}
        for n in range(len(groups) + 2):
            if n < len(groups):
                forwards[n] = [forward(*t) for t in groups[n]]
            if 0 <= n - 1 < len(groups):
                adjoints[n - 1] = [adjoint(*t, o) for t, o in zip(groups[n - 1], forwards.pop(n - 1))]
            if n >= 2:
                for t, o in zip(groups[n - 2], adjoints.pop(n - 2)):
                    finish(*t, o)

        pack(u2, 1, v)
        send(1, v)

    @pl.loop(0, variables)
    def _(v):
        load(4, v).wait()
        arrive(u2, 1, v)
        for side in (2, 3):
            guarded(side, lambda side=side: message(1, v, side).wait_send())
        for p in range(1, PASSES):
            one_pass(u2, v, p, None)

        def put(row, count, new):
            out[v, pl.ds(row - top, count)] = ct[v, pl.ds(row - top, count)] + new

        one_pass(u2, v, PASSES, put)

    @pl.loop(0, variables)
    def _(v):
        for phase in range(2):
            for side in range(8):
                if phase == 0 or side not in (2, 3):
                    guarded(side, lambda: message(phase, v, side).wait_send())

    for side in range(8):
        guarded(side, lambda side=side: coefficients(side).wait_send())


def on_device(lons, lats, control, observed, deviation, obs_weight, diffusivity, region_map, correlation):
    variables, height, width, levels = control.shape
    regions = correlation.shape[0]
    padded = (variables, height + 2 * HALO, width + 16, levels)
    pair = jnp.concatenate([diffusivity.T, obs_weight.T], axis=0)
    in_hbm = pl.BlockSpec(memory_space=pltpu.HBM)
    return pl.pallas_call(
        functools.partial(kernel, lons, lats),
        out_shape=jax.ShapeDtypeStruct(control.shape, F32),
        in_specs=[in_hbm] * 3 + [pl.BlockSpec(memory_space=pltpu.VMEM)] + [in_hbm] * 2,
        out_specs=pl.BlockSpec(memory_space=pltpu.VMEM),
        scratch_shapes=[
            pltpu.VMEM(padded, F32),
            pltpu.VMEM(padded, F32),
            pltpu.VMEM(control.shape, F32),
            pltpu.VMEM(control.shape, F32),
            pltpu.VMEM(control.shape, F32),
            pltpu.VMEM((variables, regions, levels, levels), F32),
            pltpu.VMEM((variables, regions, 2 * levels, levels), BF16),
            pltpu.VMEM((height + 2 * HALO, width + 2 * HALO, levels), F32),
            pltpu.VMEM((height + 2 * HALO, width + 2 * HALO, levels), F32),
            pltpu.VMEM((height + 2 * HALO, width + 2 * HALO, levels), F32),
            pltpu.VMEM((height + 2 * HALO, width + 2 * HALO, levels), F32),
            pltpu.VMEM((height, width, levels), F32),
            pltpu.SMEM((width, height), jnp.int32),
            pltpu.VMEM((width, 128), F32),
            pltpu.VMEM((8, width, 128), F32),
            pltpu.VMEM((2, variables, 2, height // 2, 8, levels), F32),
            pltpu.VMEM((2, variables, 4, 8, levels), F32),
            pltpu.VMEM((2, variables, 2, height // 2, 8, levels), F32),
            pltpu.VMEM((2, variables, 4, 8, levels), F32),
            pltpu.SemaphoreType.DMA((2, variables, 8)),
            pltpu.SemaphoreType.DMA((2, variables, 8)),
            pltpu.SemaphoreType.DMA((8,)),
            pltpu.SemaphoreType.DMA((8,)),
            pltpu.SemaphoreType.DMA((1,)),
            pltpu.SemaphoreType.DMA((5, variables)),
        ],
        compiler_params=pltpu.CompilerParams(
            collective_id=0, has_side_effects=True, vmem_limit_bytes=52 * 2**20),
        cost_estimate=pl.CostEstimate(flops=10**9, bytes_accessed=8 * 2**20, transcendentals=0),
    )(control, observed, deviation, pair, region_map.T, correlation)


def solution(mesh):
    field = P(None, "lat", "lon", None)
    cells = P("lat", "lon")
    return jax.shard_map(
        functools.partial(on_device, mesh.shape["lon"], mesh.shape["lat"]),
        mesh=mesh,
        in_specs=(field, field, field, cells, cells, cells, P()),
        out_specs=field,
        check_vma=False,
    )
```

```python
import functools

import jax
import jax.numpy as jnp
from jax import lax
from jax.experimental import pallas as pl
from jax.experimental.pallas import tpu as pltpu
from jax.sharding import PartitionSpec as P

PASSES = 4
HALO = 4
CHUNK = 16
GROUP = 8
MESH = pl.DeviceIdType.MESH
F32 = jnp.float32
BF16 = jnp.bfloat16

STEPS = ((-1, 0), (1, 0), (0, -1), (0, 1), (-1, -1), (1, -1), (-1, 1), (1, 1))
OPPOSITE = (1, 0, 3, 2, 7, 6, 5, 4)


def rolled(array, shift, axis):
    return pltpu.roll(array, shift % array.shape[axis], axis)


def lower_half(shape):
    return lax.broadcasted_iota(jnp.int32, shape, len(shape) - 2) < HALO


def pack_left(first, second):
    return jnp.where(lower_half(first.shape), first, rolled(second, HALO, 1))


def pack_right(first, second):
    return jnp.where(lower_half(first.shape), rolled(first, HALO, 1), second)


def corner_left(near, middle, far):
    place = lax.broadcasted_iota(jnp.int32, near.shape, 1)
    return jnp.where(place < 3, near, jnp.where(place < 5, rolled(middle, 3, 1), rolled(far, 5, 1)))


def corner_right(near, middle, far):
    place = lax.broadcasted_iota(jnp.int32, near.shape, 1)
    return jnp.where(place > 4, near, jnp.where(place > 2, rolled(middle, -3, 1), rolled(far, -5, 1)))


def halves(x):
    high = x.astype(BF16)
    return high, (x - high.astype(F32)).astype(BF16)


def kernel(
    lons, lats,
    ctl, obs, dev, cells, cor, out,
    u1, u2, ct, ob, dv, corr, split, c0, cx, cw, cy, wb, region_rows, regions, dt, dr,
    side_out, corner_out, side_in, corner_in,
    send_sem, recv_sem, dsend_sem, drecv_sem, small_sem, load_sem,
):
    variables, height, width, levels = ct.shape
    top, bottom = HALO, HALO + height
    left, right = 8, 8 + width
    me_lon, me_lat = lax.axis_index("lon"), lax.axis_index("lat")
    has_up, has_down = me_lat > 0, me_lat < lats - 1

    def neighbour(side):
        dlon, dlat = STEPS[side]
        return {"lon": lax.rem(me_lon + dlon + lons, lons), "lat": me_lat + dlat}

    def guarded(side, action):
        dlat = STEPS[side][1]
        if dlat == 0:
            action()
        else:
            pl.when(has_up if dlat < 0 else has_down)(action)

    barrier = pltpu.get_barrier_semaphore()
    for side in range(8):
        guarded(side, lambda side=side: pl.semaphore_signal(
            barrier, inc=1, device_id=neighbour(side), device_id_type=MESH))

    region_copy = pltpu.make_async_copy(region_rows, regions, small_sem.at[0])

    def own(ref, v):
        return ref.at[v, pl.ds(top, height), pl.ds(left, width)]

    def load(kind, v):
        source, target = (
            lambda: (ctl.at[v], own(u1, v)),
            lambda: (cor.at[:, v], corr.at[v]),
            lambda: (dev.at[v], dv.at[v]),
            lambda: (obs.at[v], ob.at[v]),
            lambda: (ctl.at[v], ct.at[v]),
        )[kind]()
        return pltpu.make_async_copy(source, target, load_sem.at[kind, v])

    for kind in range(4):
        for v in range(variables):
            load(kind, v).start()
    region_rows[...] = jnp.clip(cells[2 * width:3 * width].astype(jnp.int32), 0, corr.shape[1] - 1)
    region_copy.start()

    def message(phase, v, side):
        if side < 2:
            source, target = side_out.at[phase, v, side], side_in.at[phase, v, OPPOSITE[side]]
        elif side < 4:
            row = 0 if side == 2 else height - HALO
            source = ctl.at[v, pl.ds(row, HALO)] if phase == 0 else u2.at[v, pl.ds(top + row, HALO), pl.ds(left, width)]
            row = bottom if side == 2 else 0
            target = (u1 if phase == 0 else u2).at[v, pl.ds(row, HALO), pl.ds(left, width)]
        else:
            source, target = corner_out.at[phase, v, side - 4], corner_in.at[phase, v, OPPOSITE[side] - 4]
        return pltpu.make_async_remote_copy(
            source, target, send_sem.at[phase, v, side], recv_sem.at[phase, v, OPPOSITE[side]],
            device_id=neighbour(side), device_id_type=MESH)

    def arrival(phase, v, side):
        if side < 2:
            target = side_in.at[phase, v, side]
        elif side < 4:
            target = (u1 if phase == 0 else u2).at[v, pl.ds(0 if side == 2 else bottom, HALO), pl.ds(left, width)]
        else:
            target = corner_in.at[phase, v, side - 4]
        return pltpu.make_async_remote_copy(
            target, target, send_sem.at[phase, v, side], recv_sem.at[phase, v, side],
            device_id=neighbour(side), device_id_type=MESH)

    def coefficients(side):
        dlon = STEPS[side][0]
        tile = pl.ds(0 if dlon <= 0 else 8, 8 if dlon else 16)
        return pltpu.make_async_remote_copy(
            dt.at[tile], dr.at[OPPOSITE[side], tile], dsend_sem.at[side], drecv_sem.at[OPPOSITE[side]],
            device_id=neighbour(side), device_id_type=MESH)

    def coefficients_in(side):
        dlon = STEPS[side][0]
        tile = pl.ds(0 if dlon >= 0 else 8, 8 if dlon else 16)
        return pltpu.make_async_remote_copy(
            dt.at[tile], dr.at[side, tile], dsend_sem.at[side], drecv_sem.at[side],
            device_id=neighbour(side), device_id_type=MESH)

    def pack(ref, phase, v):
        half = height // 2
        for side, column, packer, corner in ((0, left, pack_left, corner_left), (1, right - 8, pack_right, corner_right)):
            columns = pl.ds(column, 8)
            side_out[phase, v, side] = packer(
                ref[v, pl.ds(top, half), columns], ref[v, pl.ds(top + half, half), columns])
            for place, rows in ((side, (top, top + 1, top + 2)), (side + 2, (bottom - 1, bottom - 2, bottom - 3))):
                corner_out[phase, v, place] = corner(*(ref[v, pl.ds(row, 1), columns] for row in rows))[0]

    def send(phase, v):
        for side in (4, 5, 6, 7, 2, 3, 0, 1):
            guarded(side, lambda side=side: message(phase, v, side).start())

    dt[...] = jnp.zeros_like(dt)
    dt[:, 0:height] = cells[0:width]
    weight_t = cells[width:2 * width]

    load(0, 0).wait()
    pack(u1, 0, 0)

    pl.semaphore_wait(barrier, 2 + 3 * has_up.astype(jnp.int32) + 3 * has_down.astype(jnp.int32))

    for side in range(8):
        guarded(side, lambda side=side: coefficients(side).start())
    send(0, 0)

    @pl.loop(1, variables)
    def _(v):
        load(0, v).wait()
        pack(u1, 0, v)
        send(0, v)

    @pl.when(jnp.logical_not(has_up))
    def _():
        for ref in (u1, u2):
            ref[:, 0:top] = jnp.zeros((variables, HALO) + ref.shape[2:], F32)
        for side in (2, 4, 5):
            dr[side] = jnp.zeros(dr.shape[1:], F32)

    @pl.when(jnp.logical_not(has_down))
    def _():
        for ref in (u1, u2):
            ref[:, bottom:bottom + HALO] = jnp.zeros((variables, HALO) + ref.shape[2:], F32)
        for side in (3, 6, 7):
            dr[side] = jnp.zeros(dr.shape[1:], F32)

    for v in range(variables):
        load(1, v).wait()

        @pl.loop(0, corr.shape[1])
        def _(r):
            high, low = halves(corr[v, r])
            split[v, r, 0:levels] = high
            split[v, r, levels:2 * levels] = low

    for side in range(8):
        guarded(side, lambda side=side: coefficients_in(side).wait_recv())

    lane = lax.broadcasted_iota(jnp.int32, (width + 16, 128), 1)

    def across(own, from_left, from_right):
        return jnp.concatenate([from_left[8:16], own[0:16], from_right[0:8]], axis=0)

    middle = across(dt, dr[0], dr[1])
    above = across(dr[2], dr[4], dr[5])
    below = across(dr[3], dr[6], dr[7])
    grid = jnp.where(lane < top, rolled(above, HALO - height, 1), 0.0)
    grid = jnp.where((lane >= top) & (lane < bottom), rolled(middle, HALO, 1), grid)
    grid = jnp.where((lane >= bottom) & (lane < bottom + HALO), rolled(below, bottom, 1), grid)
    east = 0.5 * (grid + rolled(grid, -1, 0))
    south = 0.5 * (grid + rolled(grid, -1, 1))
    rest = 1.0 - (east + rolled(east, 1, 0)) - (south + rolled(south, 1, 1))
    first_row = jnp.where(has_up, 0, top)
    last_row = jnp.where(has_down, bottom + HALO, bottom)
    inside = (lane >= first_row) & (lane < last_row)
    rest = jnp.where(inside, rest, 0.0)
    east = jnp.where(inside, east, 0.0)
    south = jnp.where(inside & (lane < last_row - 1), south, 0.0)

    kept = width + 2 * HALO
    start = left - HALO
    west = rolled(east, 1 - start, 0)[:kept]
    rest, east, south = (rolled(x, -start, 0)[:kept] for x in (rest, east, south))

    for r in range(height + 2 * HALO):
        for coefficient, ref in ((rest, c0), (east, cx), (west, cw), (south, cy)):
            ref[r] = jnp.broadcast_to(coefficient[:, r:r + 1], ref.shape[1:])
    for r in range(height):
        wb[r] = jnp.broadcast_to(weight_t[:, r:r + 1], (width, 128))

    def rows_step(ref, v, row, count, above, first, last, put):
        here_columns = pl.ds(first, last - first)
        kept_columns = pl.ds(first - start, last - first)
        block = ref[v, pl.ds(row, count + 1), here_columns]
        here = block[:count]
        up = above if count == 1 else jnp.concatenate([above, here[:-1]], axis=0)
        rows = pl.ds(row, count)
        faces = cy[pl.ds(row - 1, count + 1), kept_columns]
        new = c0[rows, kept_columns] * here + (faces[1:] * block[1:] + faces[:-1] * up)
        new = new + (cx[rows, kept_columns] * ref[v, rows, pl.ds(first + 1, last - first)]
                     + cw[rows, kept_columns] * ref[v, rows, pl.ds(first - 1, last - first)])
        put(row, count, new)
        return here[count - 1:]

    def one_pass(ref, v, p, put):
        first, last = (left - HALO, right + HALO) if p < PASSES else (left, right)
        here_columns = pl.ds(first, last - first)

        def store(row, count, new):
            ref[v, pl.ds(row, count), here_columns] = new

        above = ref[v, p - 1:p, here_columns]
        if p < PASSES:
            above = rows_step(ref, v, p, top - p, above, first, last, store)

        def chunk(k, above):
            return rows_step(ref, v, top + CHUNK * k, CHUNK, above, first, last, put or store)

        above = lax.fori_loop(0, height // CHUNK, chunk, above)
        if p < PASSES:
            rows_step(ref, v, bottom, top - p, above, first, last, store)

    def arrive(ref, phase, v):
        for side in range(8):
            guarded(side, lambda side=side: arrival(phase, v, side).wait_recv())
        half = height // 2
        to_left, to_right = pl.ds(left - 8, 8), pl.ds(right, 8)
        from_left, from_right = side_in[phase, v, 0], side_in[phase, v, 1]
        ref[v, pl.ds(top, half), to_left] = rolled(from_left, HALO, 1)
        ref[v, pl.ds(top + half, half), to_left] = from_left
        ref[v, pl.ds(top, half), to_right] = from_right
        ref[v, pl.ds(top + half, half), to_right] = rolled(from_right, HALO, 1)

        def corners(place, rows):
            for n, row in enumerate(rows):
                turn = (0, 3, 5)[n]
                ref[v, row, to_left] = rolled(corner_in[phase, v, place], turn, 0)
                ref[v, row, to_right] = rolled(corner_in[phase, v, place + 1], -turn, 0)

        pl.when(has_up)(lambda: corners(0, (top - 1, top - 2, top - 3)))
        pl.when(has_down)(lambda: corners(2, (bottom, bottom + 1, bottom + 2)))

    def joined(o):
        return o[:32, :levels] + (o[:32, levels:] + o[32:, :levels])

    region_copy.wait()
    for v in range(variables):
        load(4, v).start()

    @pl.loop(0, variables)
    def _(v):
        arrive(u1, 0, v)
        for p in range(1, PASSES + 1):
            one_pass(u1, v, p, None)
        load(2, v).wait()
        load(3, v).wait()

        def tile(ref, row, column):
            return ref[v, pl.ds(row, 4), pl.ds(column, 8)].reshape(32, levels)

        def forward(row, column):
            matrix = split[v, regions[column, row]]
            lhs = jnp.concatenate(halves(tile(u1, top + row, left + column)), axis=0)
            return lax.dot_general(lhs, matrix, (((1,), (1,)), ((), ())), preferred_element_type=F32)

        def adjoint(row, column, product):
            matrix = split[v, regions[column, row]]
            spread = tile(dv, row, column)
            weight = wb[pl.ds(row, 4), pl.ds(column, 8)].reshape(32, levels)
            weighted = spread * (weight * (spread * joined(product) - tile(ob, row, column)))
            lhs = jnp.concatenate(halves(weighted), axis=0)
            wide = jnp.concatenate([matrix[:levels], matrix[levels:]], axis=1)
            return jnp.dot(lhs, wide, preferred_element_type=F32)

        def finish(row, column, product):
            u2[v, pl.ds(top + row, 4), pl.ds(left + column, 8)] = joined(product).reshape(4, 8, levels)

        tiles = [(4 * a, 8 * b) for a in range(height // 4) for b in range(width // 8)]
        groups = [tiles[n:n + GROUP] for n in range(0, len(tiles), GROUP)]
        forwards, adjoints = {}, {}
        for n in range(len(groups) + 2):
            if n < len(groups):
                forwards[n] = [forward(*t) for t in groups[n]]
            if 0 <= n - 1 < len(groups):
                adjoints[n - 1] = [adjoint(*t, o) for t, o in zip(groups[n - 1], forwards.pop(n - 1))]
            if n >= 2:
                for t, o in zip(groups[n - 2], adjoints.pop(n - 2)):
                    finish(*t, o)

        pack(u2, 1, v)
        send(1, v)

    @pl.loop(0, variables)
    def _(v):
        load(4, v).wait()
        arrive(u2, 1, v)
        for side in (2, 3):
            guarded(side, lambda side=side: message(1, v, side).wait_send())
        for p in range(1, PASSES):
            one_pass(u2, v, p, None)

        def put(row, count, new):
            out[v, pl.ds(row - top, count)] = ct[v, pl.ds(row - top, count)] + new

        one_pass(u2, v, PASSES, put)

    @pl.loop(0, variables)
    def _(v):
        for phase in range(2):
            for side in range(8):
                if phase == 0 or side not in (2, 3):
                    guarded(side, lambda: message(phase, v, side).wait_send())

    for side in range(8):
        guarded(side, lambda side=side: coefficients(side).wait_send())


def on_device(lons, lats, control, observed, deviation, obs_weight, diffusivity, region_map, correlation):
    variables, height, width, levels = control.shape
    regions = correlation.shape[0]
    padded = (variables, height + 2 * HALO, width + 16, levels)
    cells = sum(jnp.pad(x.T, ((n * width, (2 - n) * width), (0, 0))).astype(F32) for n, x in enumerate((diffusivity, obs_weight, region_map)))
    in_hbm = pl.BlockSpec(memory_space=pltpu.HBM)
    return pl.pallas_call(
        functools.partial(kernel, lons, lats),
        out_shape=jax.ShapeDtypeStruct(control.shape, F32),
        in_specs=[in_hbm] * 3 + [pl.BlockSpec(memory_space=pltpu.VMEM)] + [in_hbm],
        out_specs=pl.BlockSpec(memory_space=pltpu.VMEM),
        scratch_shapes=[
            pltpu.VMEM(padded, F32),
            pltpu.VMEM(padded, F32),
            pltpu.VMEM(control.shape, F32),
            pltpu.VMEM(control.shape, F32),
            pltpu.VMEM(control.shape, F32),
            pltpu.VMEM((variables, regions, levels, levels), F32),
            pltpu.VMEM((variables, regions, 2 * levels, levels), BF16),
            pltpu.VMEM((height + 2 * HALO, width + 2 * HALO, levels), F32),
            pltpu.VMEM((height + 2 * HALO, width + 2 * HALO, levels), F32),
            pltpu.VMEM((height + 2 * HALO, width + 2 * HALO, levels), F32),
            pltpu.VMEM((height + 2 * HALO, width + 2 * HALO, levels), F32),
            pltpu.VMEM((height, width, levels), F32),
            pltpu.VMEM((width, height), jnp.int32),
            pltpu.SMEM((width, height), jnp.int32),
            pltpu.VMEM((width, 128), F32),
            pltpu.VMEM((8, width, 128), F32),
            pltpu.VMEM((2, variables, 2, height // 2, 8, levels), F32),
            pltpu.VMEM((2, variables, 4, 8, levels), F32),
            pltpu.VMEM((2, variables, 2, height // 2, 8, levels), F32),
            pltpu.VMEM((2, variables, 4, 8, levels), F32),
            pltpu.SemaphoreType.DMA((2, variables, 8)),
            pltpu.SemaphoreType.DMA((2, variables, 8)),
            pltpu.SemaphoreType.DMA((8,)),
            pltpu.SemaphoreType.DMA((8,)),
            pltpu.SemaphoreType.DMA((1,)),
            pltpu.SemaphoreType.DMA((5, variables)),
        ],
        compiler_params=pltpu.CompilerParams(
            collective_id=0, has_side_effects=True, vmem_limit_bytes=52 * 2**20),
        cost_estimate=pl.CostEstimate(flops=10**9, bytes_accessed=8 * 2**20, transcendentals=0),
    )(control, observed, deviation, cells, correlation)


def solution(mesh):
    field = P(None, "lat", "lon", None)
    cells = P("lat", "lon")
    return jax.shard_map(
        functools.partial(on_device, mesh.shape["lon"], mesh.shape["lat"]),
        mesh=mesh,
        in_specs=(field, field, field, cells, cells, cells, P()),
        out_specs=field,
        check_vma=False,
    )
```

```python
import functools

import jax
import jax.numpy as jnp
from jax import lax
from jax.experimental import pallas as pl
from jax.experimental.pallas import tpu as pltpu
from jax.sharding import PartitionSpec as P

PASSES = 4
HALO = 4
CHUNK = 16
GROUP = 16
MESH = pl.DeviceIdType.MESH
F32 = jnp.float32
BF16 = jnp.bfloat16

STEPS = ((-1, 0), (1, 0), (0, -1), (0, 1), (-1, -1), (1, -1), (-1, 1), (1, 1))
OPPOSITE = (1, 0, 3, 2, 7, 6, 5, 4)


def rolled(array, shift, axis):
    return pltpu.roll(array, shift % array.shape[axis], axis)


def lower_half(shape):
    return lax.broadcasted_iota(jnp.int32, shape, len(shape) - 2) < HALO


def pack_left(first, second):
    return jnp.where(lower_half(first.shape), first, rolled(second, HALO, 1))


def pack_right(first, second):
    return jnp.where(lower_half(first.shape), rolled(first, HALO, 1), second)


def corner_left(near, middle, far):
    place = lax.broadcasted_iota(jnp.int32, near.shape, 1)
    return jnp.where(place < 3, near, jnp.where(place < 5, rolled(middle, 3, 1), rolled(far, 5, 1)))


def corner_right(near, middle, far):
    place = lax.broadcasted_iota(jnp.int32, near.shape, 1)
    return jnp.where(place > 4, near, jnp.where(place > 2, rolled(middle, -3, 1), rolled(far, -5, 1)))


def halves(x):
    high = x.astype(BF16)
    return high, (x - high.astype(F32)).astype(BF16)


def kernel(
    lons, lats,
    ctl, obs, dev, cells, cor, out,
    u1, u2, ct, ob, dv, corr, split, c0, cx, cw, cy, wb, region_rows, regions, dt, dr,
    side_out, corner_out, side_in, corner_in,
    send_sem, recv_sem, dsend_sem, drecv_sem, small_sem, load_sem,
):
    variables, height, width, levels = ct.shape
    top, bottom = HALO, HALO + height
    left, right = 8, 8 + width
    me_lon, me_lat = lax.axis_index("lon"), lax.axis_index("lat")
    has_up, has_down = me_lat > 0, me_lat < lats - 1

    def neighbour(side):
        dlon, dlat = STEPS[side]
        return {"lon": lax.rem(me_lon + dlon + lons, lons), "lat": me_lat + dlat}

    def guarded(side, action):
        dlat = STEPS[side][1]
        if dlat == 0:
            action()
        else:
            pl.when(has_up if dlat < 0 else has_down)(action)

    barrier = pltpu.get_barrier_semaphore()
    for side in range(8):
        guarded(side, lambda side=side: pl.semaphore_signal(
            barrier, inc=1, device_id=neighbour(side), device_id_type=MESH))

    region_copy = pltpu.make_async_copy(region_rows, regions, small_sem.at[0])

    def own(ref, v):
        return ref.at[v, pl.ds(top, height), pl.ds(left, width)]

    def load(kind, v):
        source, target = (
            lambda: (ctl.at[v], own(u1, v)),
            lambda: (cor.at[:, v], corr.at[v]),
            lambda: (dev.at[v], dv.at[v]),
            lambda: (obs.at[v], ob.at[v]),
            lambda: (ctl.at[v], ct.at[v]),
        )[kind]()
        return pltpu.make_async_copy(source, target, load_sem.at[kind, v])

    for kind in range(4):
        for v in range(variables):
            load(kind, v).start()
    region_rows[...] = jnp.clip(cells[2 * width:3 * width].astype(jnp.int32), 0, corr.shape[1] - 1)
    region_copy.start()

    def message(phase, v, side):
        if side < 2:
            source, target = side_out.at[phase, v, side], side_in.at[phase, v, OPPOSITE[side]]
        elif side < 4:
            row = 0 if side == 2 else height - HALO
            source = ctl.at[v, pl.ds(row, HALO)] if phase == 0 else u2.at[v, pl.ds(top + row, HALO), pl.ds(left, width)]
            row = bottom if side == 2 else 0
            target = (u1 if phase == 0 else u2).at[v, pl.ds(row, HALO), pl.ds(left, width)]
        else:
            source, target = corner_out.at[phase, v, side - 4], corner_in.at[phase, v, OPPOSITE[side] - 4]
        return pltpu.make_async_remote_copy(
            source, target, send_sem.at[phase, v, side], recv_sem.at[phase, v, OPPOSITE[side]],
            device_id=neighbour(side), device_id_type=MESH)

    def arrival(phase, v, side):
        if side < 2:
            target = side_in.at[phase, v, side]
        elif side < 4:
            target = (u1 if phase == 0 else u2).at[v, pl.ds(0 if side == 2 else bottom, HALO), pl.ds(left, width)]
        else:
            target = corner_in.at[phase, v, side - 4]
        return pltpu.make_async_remote_copy(
            target, target, send_sem.at[phase, v, side], recv_sem.at[phase, v, side],
            device_id=neighbour(side), device_id_type=MESH)

    def coefficients(side):
        dlon = STEPS[side][0]
        tile = pl.ds(0 if dlon <= 0 else 8, 8 if dlon else 16)
        return pltpu.make_async_remote_copy(
            dt.at[tile], dr.at[OPPOSITE[side], tile], dsend_sem.at[side], drecv_sem.at[OPPOSITE[side]],
            device_id=neighbour(side), device_id_type=MESH)

    def coefficients_in(side):
        dlon = STEPS[side][0]
        tile = pl.ds(0 if dlon >= 0 else 8, 8 if dlon else 16)
        return pltpu.make_async_remote_copy(
            dt.at[tile], dr.at[side, tile], dsend_sem.at[side], drecv_sem.at[side],
            device_id=neighbour(side), device_id_type=MESH)

    def pack(ref, phase, v):
        half = height // 2
        for side, column, packer, corner in ((0, left, pack_left, corner_left), (1, right - 8, pack_right, corner_right)):
            columns = pl.ds(column, 8)
            side_out[phase, v, side] = packer(
                ref[v, pl.ds(top, half), columns], ref[v, pl.ds(top + half, half), columns])
            for place, rows in ((side, (top, top + 1, top + 2)), (side + 2, (bottom - 1, bottom - 2, bottom - 3))):
                corner_out[phase, v, place] = corner(*(ref[v, pl.ds(row, 1), columns] for row in rows))[0]

    def send(phase, v):
        for side in (4, 5, 6, 7, 2, 3, 0, 1):
            guarded(side, lambda side=side: message(phase, v, side).start())

    dt[...] = jnp.zeros_like(dt)
    dt[:, 0:height] = cells[0:width]
    weight_t = cells[width:2 * width]

    load(0, 0).wait()
    pack(u1, 0, 0)

    pl.semaphore_wait(barrier, 2 + 3 * has_up.astype(jnp.int32) + 3 * has_down.astype(jnp.int32))

    for side in range(8):
        guarded(side, lambda side=side: coefficients(side).start())
    send(0, 0)

    @pl.loop(1, variables)
    def _(v):
        load(0, v).wait()
        pack(u1, 0, v)
        send(0, v)

    @pl.when(jnp.logical_not(has_up))
    def _():
        for ref in (u1, u2):
            ref[:, 0:top] = jnp.zeros((variables, HALO) + ref.shape[2:], F32)
        for side in (2, 4, 5):
            dr[side] = jnp.zeros(dr.shape[1:], F32)

    @pl.when(jnp.logical_not(has_down))
    def _():
        for ref in (u1, u2):
            ref[:, bottom:bottom + HALO] = jnp.zeros((variables, HALO) + ref.shape[2:], F32)
        for side in (3, 6, 7):
            dr[side] = jnp.zeros(dr.shape[1:], F32)

    for v in range(variables):
        load(1, v).wait()

        @pl.loop(0, corr.shape[1])
        def _(r):
            high, low = halves(corr[v, r])
            split[v, r, 0:levels] = high
            split[v, r, levels:2 * levels] = low

    for side in range(8):
        guarded(side, lambda side=side: coefficients_in(side).wait_recv())

    lane = lax.broadcasted_iota(jnp.int32, (width + 16, 128), 1)

    def across(own, from_left, from_right):
        return jnp.concatenate([from_left[8:16], own[0:16], from_right[0:8]], axis=0)

    middle = across(dt, dr[0], dr[1])
    above = across(dr[2], dr[4], dr[5])
    below = across(dr[3], dr[6], dr[7])
    grid = jnp.where(lane < top, rolled(above, HALO - height, 1), 0.0)
    grid = jnp.where((lane >= top) & (lane < bottom), rolled(middle, HALO, 1), grid)
    grid = jnp.where((lane >= bottom) & (lane < bottom + HALO), rolled(below, bottom, 1), grid)
    east = 0.5 * (grid + rolled(grid, -1, 0))
    south = 0.5 * (grid + rolled(grid, -1, 1))
    rest = 1.0 - (east + rolled(east, 1, 0)) - (south + rolled(south, 1, 1))
    first_row = jnp.where(has_up, 0, top)
    last_row = jnp.where(has_down, bottom + HALO, bottom)
    inside = (lane >= first_row) & (lane < last_row)
    rest = jnp.where(inside, rest, 0.0)
    east = jnp.where(inside, east, 0.0)
    south = jnp.where(inside & (lane < last_row - 1), south, 0.0)

    kept = width + 2 * HALO
    start = left - HALO
    west = rolled(east, 1 - start, 0)[:kept]
    rest, east, south = (rolled(x, -start, 0)[:kept] for x in (rest, east, south))

    for r in range(height + 2 * HALO):
        for coefficient, ref in ((rest, c0), (east, cx), (west, cw), (south, cy)):
            ref[r] = jnp.broadcast_to(coefficient[:, r:r + 1], ref.shape[1:])
    for r in range(height):
        wb[r] = jnp.broadcast_to(weight_t[:, r:r + 1], (width, 128))

    def rows_step(ref, v, row, count, above, first, last, put):
        here_columns = pl.ds(first, last - first)
        kept_columns = pl.ds(first - start, last - first)
        block = ref[v, pl.ds(row, count + 1), here_columns]
        here = block[:count]
        up = above if count == 1 else jnp.concatenate([above, here[:-1]], axis=0)
        rows = pl.ds(row, count)
        faces = cy[pl.ds(row - 1, count + 1), kept_columns]
        new = c0[rows, kept_columns] * here + (faces[1:] * block[1:] + faces[:-1] * up)
        new = new + (cx[rows, kept_columns] * ref[v, rows, pl.ds(first + 1, last - first)]
                     + cw[rows, kept_columns] * ref[v, rows, pl.ds(first - 1, last - first)])
        put(row, count, new)
        return here[count - 1:]

    def one_pass(ref, v, p, put):
        first, last = (left - HALO, right + HALO) if p < PASSES else (left, right)
        here_columns = pl.ds(first, last - first)

        def store(row, count, new):
            ref[v, pl.ds(row, count), here_columns] = new

        above = ref[v, p - 1:p, here_columns]
        if p < PASSES:
            above = rows_step(ref, v, p, top - p, above, first, last, store)

        def chunk(k, above):
            return rows_step(ref, v, top + CHUNK * k, CHUNK, above, first, last, put or store)

        above = lax.fori_loop(0, height // CHUNK, chunk, above)
        if p < PASSES:
            rows_step(ref, v, bottom, top - p, above, first, last, store)

    def arrive(ref, phase, v):
        for side in range(8):
            guarded(side, lambda side=side: arrival(phase, v, side).wait_recv())
        half = height // 2
        to_left, to_right = pl.ds(left - 8, 8), pl.ds(right, 8)
        from_left, from_right = side_in[phase, v, 0], side_in[phase, v, 1]
        ref[v, pl.ds(top, half), to_left] = rolled(from_left, HALO, 1)
        ref[v, pl.ds(top + half, half), to_left] = from_left
        ref[v, pl.ds(top, half), to_right] = from_right
        ref[v, pl.ds(top + half, half), to_right] = rolled(from_right, HALO, 1)

        def corners(place, rows):
            for n, row in enumerate(rows):
                turn = (0, 3, 5)[n]
                ref[v, row, to_left] = rolled(corner_in[phase, v, place], turn, 0)
                ref[v, row, to_right] = rolled(corner_in[phase, v, place + 1], -turn, 0)

        pl.when(has_up)(lambda: corners(0, (top - 1, top - 2, top - 3)))
        pl.when(has_down)(lambda: corners(2, (bottom, bottom + 1, bottom + 2)))

    def joined(o):
        return o[:32, :levels] + (o[:32, levels:] + o[32:, :levels])

    region_copy.wait()
    for v in range(variables):
        load(4, v).start()

    @pl.loop(0, variables)
    def _(v):
        arrive(u1, 0, v)
        for p in range(1, PASSES + 1):
            one_pass(u1, v, p, None)
        load(2, v).wait()
        load(3, v).wait()

        def tile(ref, row, column):
            return ref[v, pl.ds(row, 4), pl.ds(column, 8)].reshape(32, levels)

        def forward(row, column):
            matrix = split[v, regions[column, row]]
            lhs = jnp.concatenate(halves(tile(u1, top + row, left + column)), axis=0)
            return lax.dot_general(lhs, matrix, (((1,), (1,)), ((), ())), preferred_element_type=F32)

        def adjoint(row, column, product):
            matrix = split[v, regions[column, row]]
            spread = tile(dv, row, column)
            weight = wb[pl.ds(row, 4), pl.ds(column, 8)].reshape(32, levels)
            weighted = spread * (weight * (spread * joined(product) - tile(ob, row, column)))
            lhs = jnp.concatenate(halves(weighted), axis=0)
            wide = jnp.concatenate([matrix[:levels], matrix[levels:]], axis=1)
            return jnp.dot(lhs, wide, preferred_element_type=F32)

        def finish(row, column, product):
            u2[v, pl.ds(top + row, 4), pl.ds(left + column, 8)] = joined(product).reshape(4, 8, levels)

        tiles = [(4 * a, 8 * b) for a in range(height // 4) for b in range(width // 8)]
        groups = [tiles[n:n + GROUP] for n in range(0, len(tiles), GROUP)]
        forwards, adjoints = {}, {}
        for n in range(len(groups) + 2):
            if n < len(groups):
                forwards[n] = [forward(*t) for t in groups[n]]
            if 0 <= n - 1 < len(groups):
                adjoints[n - 1] = [adjoint(*t, o) for t, o in zip(groups[n - 1], forwards.pop(n - 1))]
            if n >= 2:
                for t, o in zip(groups[n - 2], adjoints.pop(n - 2)):
                    finish(*t, o)

        pack(u2, 1, v)
        send(1, v)

    @pl.loop(0, variables)
    def _(v):
        load(4, v).wait()
        arrive(u2, 1, v)
        for side in (2, 3):
            guarded(side, lambda side=side: message(1, v, side).wait_send())
        for p in range(1, PASSES):
            one_pass(u2, v, p, None)

        def put(row, count, new):
            out[v, pl.ds(row - top, count)] = ct[v, pl.ds(row - top, count)] + new

        one_pass(u2, v, PASSES, put)

    @pl.loop(0, variables)
    def _(v):
        for phase in range(2):
            for side in range(8):
                if phase == 0 or side not in (2, 3):
                    guarded(side, lambda: message(phase, v, side).wait_send())

    for side in range(8):
        guarded(side, lambda side=side: coefficients(side).wait_send())


def on_device(lons, lats, control, observed, deviation, obs_weight, diffusivity, region_map, correlation):
    variables, height, width, levels = control.shape
    regions = correlation.shape[0]
    padded = (variables, height + 2 * HALO, width + 16, levels)
    cells = sum(jnp.pad(x.T, ((n * width, (2 - n) * width), (0, 0))).astype(F32) for n, x in enumerate((diffusivity, obs_weight, region_map)))
    in_hbm = pl.BlockSpec(memory_space=pltpu.HBM)
    return pl.pallas_call(
        functools.partial(kernel, lons, lats),
        out_shape=jax.ShapeDtypeStruct(control.shape, F32),
        in_specs=[in_hbm] * 3 + [pl.BlockSpec(memory_space=pltpu.VMEM)] + [in_hbm],
        out_specs=pl.BlockSpec(memory_space=pltpu.VMEM),
        scratch_shapes=[
            pltpu.VMEM(padded, F32),
            pltpu.VMEM(padded, F32),
            pltpu.VMEM(control.shape, F32),
            pltpu.VMEM(control.shape, F32),
            pltpu.VMEM(control.shape, F32),
            pltpu.VMEM((variables, regions, levels, levels), F32),
            pltpu.VMEM((variables, regions, 2 * levels, levels), BF16),
            pltpu.VMEM((height + 2 * HALO, width + 2 * HALO, levels), F32),
            pltpu.VMEM((height + 2 * HALO, width + 2 * HALO, levels), F32),
            pltpu.VMEM((height + 2 * HALO, width + 2 * HALO, levels), F32),
            pltpu.VMEM((height + 2 * HALO, width + 2 * HALO, levels), F32),
            pltpu.VMEM((height, width, levels), F32),
            pltpu.VMEM((width, height), jnp.int32),
            pltpu.SMEM((width, height), jnp.int32),
            pltpu.VMEM((width, 128), F32),
            pltpu.VMEM((8, width, 128), F32),
            pltpu.VMEM((2, variables, 2, height // 2, 8, levels), F32),
            pltpu.VMEM((2, variables, 4, 8, levels), F32),
            pltpu.VMEM((2, variables, 2, height // 2, 8, levels), F32),
            pltpu.VMEM((2, variables, 4, 8, levels), F32),
            pltpu.SemaphoreType.DMA((2, variables, 8)),
            pltpu.SemaphoreType.DMA((2, variables, 8)),
            pltpu.SemaphoreType.DMA((8,)),
            pltpu.SemaphoreType.DMA((8,)),
            pltpu.SemaphoreType.DMA((1,)),
            pltpu.SemaphoreType.DMA((5, variables)),
        ],
        compiler_params=pltpu.CompilerParams(
            collective_id=0, has_side_effects=True, vmem_limit_bytes=52 * 2**20),
        cost_estimate=pl.CostEstimate(flops=10**9, bytes_accessed=8 * 2**20, transcendentals=0),
    )(control, observed, deviation, cells, correlation)


def solution(mesh):
    field = P(None, "lat", "lon", None)
    cells = P("lat", "lon")
    return jax.shard_map(
        functools.partial(on_device, mesh.shape["lon"], mesh.shape["lat"]),
        mesh=mesh,
        in_specs=(field, field, field, cells, cells, cells, P()),
        out_specs=field,
        check_vma=False,
    )
```

```python
import functools

import jax
import jax.numpy as jnp
from jax import lax
from jax.experimental import pallas as pl
from jax.experimental.pallas import tpu as pltpu
from jax.sharding import PartitionSpec as P

PASSES = 4
HALO = 4
CHUNK = 16
GROUP = 8
MESH = pl.DeviceIdType.MESH
F32 = jnp.float32
BF16 = jnp.bfloat16

STEPS = ((-1, 0), (1, 0), (0, -1), (0, 1), (-1, -1), (1, -1), (-1, 1), (1, 1))
OPPOSITE = (1, 0, 3, 2, 7, 6, 5, 4)


def rolled(array, shift, axis):
    return pltpu.roll(array, shift % array.shape[axis], axis)


def lower_half(shape):
    return lax.broadcasted_iota(jnp.int32, shape, len(shape) - 2) < HALO


def pack_left(first, second):
    return jnp.where(lower_half(first.shape), first, rolled(second, HALO, 1))


def pack_right(first, second):
    return jnp.where(lower_half(first.shape), rolled(first, HALO, 1), second)


def corner_left(near, middle, far):
    place = lax.broadcasted_iota(jnp.int32, near.shape, 1)
    return jnp.where(place < 3, near, jnp.where(place < 5, rolled(middle, 3, 1), rolled(far, 5, 1)))


def corner_right(near, middle, far):
    place = lax.broadcasted_iota(jnp.int32, near.shape, 1)
    return jnp.where(place > 4, near, jnp.where(place > 2, rolled(middle, -3, 1), rolled(far, -5, 1)))


def halves(x):
    high = x.astype(BF16)
    return high, (x - high.astype(F32)).astype(BF16)


def kernel(
    lons, lats,
    ctl, obs, dev, cells, cor, out,
    u1, u2, ct, ob, dv, corr, split, c0, cx, cw, cy, wb, region_rows, regions, dt, dr,
    side_out, corner_out, side_in, corner_in,
    send_sem, recv_sem, dsend_sem, drecv_sem, small_sem, load_sem,
):
    variables, height, width, levels = ct.shape
    top, bottom = HALO, HALO + height
    left, right = 8, 8 + width
    me_lon, me_lat = lax.axis_index("lon"), lax.axis_index("lat")
    has_up, has_down = me_lat > 0, me_lat < lats - 1

    def neighbour(side):
        dlon, dlat = STEPS[side]
        return {"lon": lax.rem(me_lon + dlon + lons, lons), "lat": me_lat + dlat}

    def guarded(side, action):
        dlat = STEPS[side][1]
        if dlat == 0:
            action()
        else:
            pl.when(has_up if dlat < 0 else has_down)(action)

    barrier = pltpu.get_barrier_semaphore()
    for side in range(8):
        guarded(side, lambda side=side: pl.semaphore_signal(
            barrier, inc=1, device_id=neighbour(side), device_id_type=MESH))

    region_copy = pltpu.make_async_copy(region_rows, regions, small_sem.at[0])

    def own(ref, v):
        return ref.at[v, pl.ds(top, height), pl.ds(left, width)]

    def load(kind, v):
        source, target = (
            lambda: (ctl.at[v], own(u1, v)),
            lambda: (cor.at[:, v], corr.at[v]),
            lambda: (dev.at[v], dv.at[v]),
            lambda: (obs.at[v], ob.at[v]),
            lambda: (ctl.at[v], ct.at[v]),
        )[kind]()
        return pltpu.make_async_copy(source, target, load_sem.at[kind, v])

    for kind in range(4):
        for v in range(variables):
            load(kind, v).start()
    region_rows[...] = jnp.clip(cells[2 * width:3 * width].astype(jnp.int32), 0, corr.shape[1] - 1)
    region_copy.start()

    def message(phase, v, side):
        if side < 2:
            source, target = side_out.at[phase, v, side], side_in.at[phase, v, OPPOSITE[side]]
        elif side < 4:
            row = 0 if side == 2 else height - HALO
            source = ctl.at[v, pl.ds(row, HALO)] if phase == 0 else u2.at[v, pl.ds(top + row, HALO), pl.ds(left, width)]
            row = bottom if side == 2 else 0
            target = (u1 if phase == 0 else u2).at[v, pl.ds(row, HALO), pl.ds(left, width)]
        else:
            source, target = corner_out.at[phase, v, side - 4], corner_in.at[phase, v, OPPOSITE[side] - 4]
        return pltpu.make_async_remote_copy(
            source, target, send_sem.at[phase, v, side], recv_sem.at[phase, v, OPPOSITE[side]],
            device_id=neighbour(side), device_id_type=MESH)

    def arrival(phase, v, side):
        if side < 2:
            target = side_in.at[phase, v, side]
        elif side < 4:
            target = (u1 if phase == 0 else u2).at[v, pl.ds(0 if side == 2 else bottom, HALO), pl.ds(left, width)]
        else:
            target = corner_in.at[phase, v, side - 4]
        return pltpu.make_async_remote_copy(
            target, target, send_sem.at[phase, v, side], recv_sem.at[phase, v, side],
            device_id=neighbour(side), device_id_type=MESH)

    def coefficients(side):
        dlon = STEPS[side][0]
        tile = pl.ds(0 if dlon <= 0 else 8, 8 if dlon else 16)
        return pltpu.make_async_remote_copy(
            dt.at[tile], dr.at[OPPOSITE[side], tile], dsend_sem.at[side], drecv_sem.at[OPPOSITE[side]],
            device_id=neighbour(side), device_id_type=MESH)

    def coefficients_in(side):
        dlon = STEPS[side][0]
        tile = pl.ds(0 if dlon >= 0 else 8, 8 if dlon else 16)
        return pltpu.make_async_remote_copy(
            dt.at[tile], dr.at[side, tile], dsend_sem.at[side], drecv_sem.at[side],
            device_id=neighbour(side), device_id_type=MESH)

    def pack(ref, phase, v):
        half = height // 2
        for side, column, packer, corner in ((0, left, pack_left, corner_left), (1, right - 8, pack_right, corner_right)):
            columns = pl.ds(column, 8)
            side_out[phase, v, side] = packer(
                ref[v, pl.ds(top, half), columns], ref[v, pl.ds(top + half, half), columns])
            for place, rows in ((side, (top, top + 1, top + 2)), (side + 2, (bottom - 1, bottom - 2, bottom - 3))):
                corner_out[phase, v, place] = corner(*(ref[v, pl.ds(row, 1), columns] for row in rows))[0]

    def send(phase, v):
        for side in (4, 5, 6, 7, 2, 3, 0, 1):
            guarded(side, lambda side=side: message(phase, v, side).start())

    dt[...] = jnp.zeros_like(dt)
    dt[:, 0:height] = cells[0:width]
    weight_t = cells[width:2 * width]

    load(0, 0).wait()
    pack(u1, 0, 0)

    pl.semaphore_wait(barrier, 2 + 3 * has_up.astype(jnp.int32) + 3 * has_down.astype(jnp.int32))

    for side in range(8):
        guarded(side, lambda side=side: coefficients(side).start())
    send(0, 0)

    @pl.loop(1, variables)
    def _(v):
        load(0, v).wait()
        pack(u1, 0, v)
        send(0, v)

    @pl.when(jnp.logical_not(has_up))
    def _():
        for ref in (u1, u2):
            ref[:, 0:top] = jnp.zeros((variables, HALO) + ref.shape[2:], F32)
        for side in (2, 4, 5):
            dr[side] = jnp.zeros(dr.shape[1:], F32)

    @pl.when(jnp.logical_not(has_down))
    def _():
        for ref in (u1, u2):
            ref[:, bottom:bottom + HALO] = jnp.zeros((variables, HALO) + ref.shape[2:], F32)
        for side in (3, 6, 7):
            dr[side] = jnp.zeros(dr.shape[1:], F32)

    for v in range(variables):
        load(1, v).wait()

        @pl.loop(0, corr.shape[1])
        def _(r):
            high, low = halves(corr[v, r])
            split[v, r, 0:levels] = high
            split[v, r, levels:2 * levels] = low

    for side in range(8):
        guarded(side, lambda side=side: coefficients_in(side).wait_recv())

    lane = lax.broadcasted_iota(jnp.int32, (width + 16, 128), 1)

    def across(own, from_left, from_right):
        return jnp.concatenate([from_left[8:16], own[0:16], from_right[0:8]], axis=0)

    middle = across(dt, dr[0], dr[1])
    above = across(dr[2], dr[4], dr[5])
    below = across(dr[3], dr[6], dr[7])
    grid = jnp.where(lane < top, rolled(above, HALO - height, 1), 0.0)
    grid = jnp.where((lane >= top) & (lane < bottom), rolled(middle, HALO, 1), grid)
    grid = jnp.where((lane >= bottom) & (lane < bottom + HALO), rolled(below, bottom, 1), grid)
    east = 0.5 * (grid + rolled(grid, -1, 0))
    south = 0.5 * (grid + rolled(grid, -1, 1))
    rest = 1.0 - (east + rolled(east, 1, 0)) - (south + rolled(south, 1, 1))
    first_row = jnp.where(has_up, 0, top)
    last_row = jnp.where(has_down, bottom + HALO, bottom)
    inside = (lane >= first_row) & (lane < last_row)
    rest = jnp.where(inside, rest, 0.0)
    east = jnp.where(inside, east, 0.0)
    south = jnp.where(inside & (lane < last_row - 1), south, 0.0)

    kept = width + 2 * HALO
    start = left - HALO
    west = rolled(east, 1 - start, 0)[:kept]
    rest, east, south = (rolled(x, -start, 0)[:kept] for x in (rest, east, south))

    for r in range(height + 2 * HALO):
        for coefficient, ref in ((rest, c0), (east, cx), (west, cw), (south, cy)):
            ref[r] = jnp.broadcast_to(coefficient[:, r:r + 1], ref.shape[1:])
    for r in range(height):
        wb[r] = jnp.broadcast_to(weight_t[:, r:r + 1], (width, 128))

    def rows_step(ref, v, row, count, above, first, last, put):
        here_columns = pl.ds(first, last - first)
        kept_columns = pl.ds(first - start, last - first)
        block = ref[v, pl.ds(row, count + 1), here_columns]
        here = block[:count]
        up = above if count == 1 else jnp.concatenate([above, here[:-1]], axis=0)
        rows = pl.ds(row, count)
        faces = cy[pl.ds(row - 1, count + 1), kept_columns]
        new = c0[rows, kept_columns] * here + (faces[1:] * block[1:] + faces[:-1] * up)
        new = new + (cx[rows, kept_columns] * ref[v, rows, pl.ds(first + 1, last - first)]
                     + cw[rows, kept_columns] * ref[v, rows, pl.ds(first - 1, last - first)])
        put(row, count, new)
        return here[count - 1:]

    def one_pass(ref, v, p, put):
        first, last = (left - HALO, right + HALO) if p < PASSES else (left, right)
        here_columns = pl.ds(first, last - first)

        def store(row, count, new):
            ref[v, pl.ds(row, count), here_columns] = new

        above = ref[v, p - 1:p, here_columns]
        if p < PASSES:
            above = rows_step(ref, v, p, top - p, above, first, last, store)

        def chunk(k, above):
            return rows_step(ref, v, top + CHUNK * k, CHUNK, above, first, last, put or store)

        above = lax.fori_loop(0, height // CHUNK, chunk, above)
        if p < PASSES:
            rows_step(ref, v, bottom, top - p, above, first, last, store)

    def arrive(ref, phase, v):
        for side in range(8):
            guarded(side, lambda side=side: arrival(phase, v, side).wait_recv())
        half = height // 2
        to_left, to_right = pl.ds(left - 8, 8), pl.ds(right, 8)
        from_left, from_right = side_in[phase, v, 0], side_in[phase, v, 1]
        ref[v, pl.ds(top, half), to_left] = rolled(from_left, HALO, 1)
        ref[v, pl.ds(top + half, half), to_left] = from_left
        ref[v, pl.ds(top, half), to_right] = from_right
        ref[v, pl.ds(top + half, half), to_right] = rolled(from_right, HALO, 1)

        def corners(place, rows):
            for n, row in enumerate(rows):
                turn = (0, 3, 5)[n]
                ref[v, row, to_left] = rolled(corner_in[phase, v, place], turn, 0)
                ref[v, row, to_right] = rolled(corner_in[phase, v, place + 1], -turn, 0)

        pl.when(has_up)(lambda: corners(0, (top - 1, top - 2, top - 3)))
        pl.when(has_down)(lambda: corners(2, (bottom, bottom + 1, bottom + 2)))

    def joined(o):
        return o[:32, :levels] + (o[:32, levels:] + o[32:, :levels])

    region_copy.wait()
    for v in range(variables):
        load(4, v).start()

    @pl.loop(0, variables)
    def _(v):
        arrive(u1, 0, v)
        for p in range(1, PASSES + 1):
            one_pass(u1, v, p, None)
        load(2, v).wait()
        load(3, v).wait()

        def tile(ref, row, column):
            return ref[v, pl.ds(row, 4), pl.ds(column, 8)].reshape(32, levels)

        def forward(row, column):
            matrix = split[v, regions[column, row]]
            lhs = jnp.concatenate(halves(tile(u1, top + row, left + column)), axis=0)
            return lax.dot_general(lhs, matrix, (((1,), (1,)), ((), ())), preferred_element_type=F32)

        def adjoint(row, column, product):
            matrix = split[v, regions[column, row]]
            spread = tile(dv, row, column)
            weight = wb[pl.ds(row, 4), pl.ds(column, 8)].reshape(32, levels)
            weighted = spread * (weight * (spread * joined(product) - tile(ob, row, column)))
            lhs = jnp.concatenate(halves(weighted), axis=0)
            wide = jnp.concatenate([matrix[:levels], matrix[levels:]], axis=1)
            return jnp.dot(lhs, wide, preferred_element_type=F32)

        def finish(row, column, product):
            u2[v, pl.ds(top + row, 4), pl.ds(left + column, 8)] = joined(product).reshape(4, 8, levels)

        tiles = [(4 * a, 8 * b) for a in range(height // 4) for b in range(width // 8)]
        groups = [tiles[n:n + GROUP] for n in range(0, len(tiles), GROUP)]
        forwards, adjoints = {}, {}
        for n in range(len(groups) + 2):
            if n < len(groups):
                forwards[n] = [forward(*t) for t in groups[n]]
            if 0 <= n - 1 < len(groups):
                adjoints[n - 1] = [adjoint(*t, o) for t, o in zip(groups[n - 1], forwards.pop(n - 1))]
            if n >= 2:
                for t, o in zip(groups[n - 2], adjoints.pop(n - 2)):
                    finish(*t, o)

        pack(u2, 1, v)
        send(1, v)

    @pl.loop(0, variables)
    def _(v):
        load(4, v).wait()
        for side in range(8):
            guarded(side, lambda side=side: message(0, v, side).wait_send())
        arrive(u2, 1, v)
        for side in (2, 3):
            guarded(side, lambda side=side: message(1, v, side).wait_send())
        for p in range(1, PASSES):
            one_pass(u2, v, p, None)

        def put(row, count, new):
            out[v, pl.ds(row - top, count)] = ct[v, pl.ds(row - top, count)] + new

        one_pass(u2, v, PASSES, put)

    @pl.loop(0, variables)
    def _(v):
        for side in (0, 1, 4, 5, 6, 7):
            guarded(side, lambda side=side: message(1, v, side).wait_send())

    for side in range(8):
        guarded(side, lambda side=side: coefficients(side).wait_send())


def on_device(lons, lats, control, observed, deviation, obs_weight, diffusivity, region_map, correlation):
    variables, height, width, levels = control.shape
    regions = correlation.shape[0]
    padded = (variables, height + 2 * HALO, width + 16, levels)
    cells = sum(jnp.pad(x.T, ((n * width, (2 - n) * width), (0, 0))).astype(F32) for n, x in enumerate((diffusivity, obs_weight, region_map)))
    in_hbm = pl.BlockSpec(memory_space=pltpu.HBM)
    return pl.pallas_call(
        functools.partial(kernel, lons, lats),
        out_shape=jax.ShapeDtypeStruct(control.shape, F32),
        in_specs=[in_hbm] * 3 + [pl.BlockSpec(memory_space=pltpu.VMEM)] + [in_hbm],
        out_specs=pl.BlockSpec(memory_space=pltpu.VMEM),
        scratch_shapes=[
            pltpu.VMEM(padded, F32),
            pltpu.VMEM(padded, F32),
            pltpu.VMEM(control.shape, F32),
            pltpu.VMEM(control.shape, F32),
            pltpu.VMEM(control.shape, F32),
            pltpu.VMEM((variables, regions, levels, levels), F32),
            pltpu.VMEM((variables, regions, 2 * levels, levels), BF16),
            pltpu.VMEM((height + 2 * HALO, width + 2 * HALO, levels), F32),
            pltpu.VMEM((height + 2 * HALO, width + 2 * HALO, levels), F32),
            pltpu.VMEM((height + 2 * HALO, width + 2 * HALO, levels), F32),
            pltpu.VMEM((height + 2 * HALO, width + 2 * HALO, levels), F32),
            pltpu.VMEM((height, width, levels), F32),
            pltpu.VMEM((width, height), jnp.int32),
            pltpu.SMEM((width, height), jnp.int32),
            pltpu.VMEM((width, 128), F32),
            pltpu.VMEM((8, width, 128), F32),
            pltpu.VMEM((2, variables, 2, height // 2, 8, levels), F32),
            pltpu.VMEM((2, variables, 4, 8, levels), F32),
            pltpu.VMEM((2, variables, 2, height // 2, 8, levels), F32),
            pltpu.VMEM((2, variables, 4, 8, levels), F32),
            pltpu.SemaphoreType.DMA((2, variables, 8)),
            pltpu.SemaphoreType.DMA((2, variables, 8)),
            pltpu.SemaphoreType.DMA((8,)),
            pltpu.SemaphoreType.DMA((8,)),
            pltpu.SemaphoreType.DMA((1,)),
            pltpu.SemaphoreType.DMA((5, variables)),
        ],
        compiler_params=pltpu.CompilerParams(
            collective_id=0, has_side_effects=True, vmem_limit_bytes=52 * 2**20),
        cost_estimate=pl.CostEstimate(flops=10**9, bytes_accessed=8 * 2**20, transcendentals=0),
    )(control, observed, deviation, cells, correlation)


def solution(mesh):
    field = P(None, "lat", "lon", None)
    cells = P("lat", "lon")
    return jax.shard_map(
        functools.partial(on_device, mesh.shape["lon"], mesh.shape["lat"]),
        mesh=mesh,
        in_specs=(field, field, field, cells, cells, cells, P()),
        out_specs=field,
        check_vma=False,
    )
```
